32 devices in a mesh: freq: 8 (over z, y), chan: 2 (over x), expert: 2 (over core).
Axes of the slice: x: 2, y: 2, z: 4, core: 2. Of those that a mesh axis runs over, the one named last changes fastest.
Arguments:
- spectra: bfloat16 [2048, 1024], P('freq', ('chan', 'expert')), may hold values from -6 to 6
- spectral_filter: bfloat16 [2, 256, 8, 1024], P(None, None, 'freq', ('chan', 'expert')), may hold values from -5 to 5
- norm_gain: float32 [1024], replicated, may hold values from 0.1 to 1.9
- mlp_gate: bfloat16 [1024, 2048], P(None, ('chan', 'expert')), may hold values from -0.1875 to 0.1875
- mlp_up: bfloat16 [1024, 2048], P(None, ('chan', 'expert')), may hold values from -0.1875 to 0.1875
- mlp_down: bfloat16 [2048, 1024], P(('chan', 'expert')), may hold values from -0.125 to 0.125
- expert_gain: float32 [1024], replicated, may hold values from 0.1 to 1.9
- expert_gate: bfloat16 [8, 1024, 4096], P('freq', None, ('chan', 'expert')), may hold values from -0.1875 to 0.1875
- expert_up: bfloat16 [8, 1024, 4096], P('freq', None, ('chan', 'expert')), may hold values from -0.1875 to 0.1875
- expert_down: bfloat16 [8, 4096, 1024], P('freq', ('chan', 'expert')), may hold values from -0.09375 to 0.09375
- routes: int32 [2048, 2], P('freq'), may hold values from 0 to 7, all different within a row; in each aligned block of 256 rows (0 to 255, 256 to 511, ...) at most 128 rows name the same one
- combine: int32 [2048, 2], P('freq'), may hold values from 1 to 8
Outputs:
- layer_out: bfloat16 [2048, 1024], P('freq', ('chan', 'expert'))
The draws below stay inside these ranges and needn't reach their ends.
Inputs may be any that keep to these rules, and one draw needn't show every extreme that they name: `routes`: in each aligned block of 256 rows (the rows of one device) no expert is named by more than 128 rows, a bound that some block reaches; the two experts of a row differ.
All inputs are finite; a program needn't handle non-finite values.
Results may differ from the reference program's by a relative error of at most 0.015.
Values may be sent and summed in bfloat16 or wider, within the bound.
A program may use at most 64 MiB of HBM per device.

```python
import math
import jax
import jax.numpy as jnp
import numpy as np
from jax import lax

D = 1024
FF_ENC = 2048
FFE = 4096
TOP = 2
POINTS_DEV = 256
POINTS = 2048
EXPERTS = 8
CAP = 128
N_FREQ = 8
N_CHAN = 2
N_EXPERT = 2


def set_ends(entries, own_key, smallest, high):
    place = [jax.random.randint(jax.random.fold_in(own_key, axis), (), 0, length) for axis, length in enumerate(entries.shape)]
    longest = entries.shape.index(max(entries.shape))
    next_to = place[:longest] + [(place[longest] + 1) % entries.shape[longest]] + place[longest + 1:]
    return entries.at[tuple(place)].set(smallest).at[tuple(next_to)].set(high)


def block_levels(rng, shape, cuts, low, high):
    factor_of, own = 1.0, jax.random.fold_in(rng, 6)
    for axis_at, blocks in cuts:
        steps = jnp.exp(jax.random.uniform(jax.random.fold_in(own, axis_at), (blocks,), jnp.float32, low / len(cuts), high / len(cuts)))
        factor_of = factor_of * jnp.repeat(steps, shape[axis_at] // blocks).reshape([-1 if axis == axis_at else 1 for axis in range(len(shape))])
    return factor_of


def assign_block(own_key, own, number, rows, amount, top, bound, lean):
    ranking = jax.random.permutation(own_key, amount)
    packed, common = portions_of(amount, rows * top, bound, lean, True), portions_of(amount, rows * top, bound, lean, False)
    places = jnp.arange(amount)

    def named(tallies, rotation):
        used = int((tallies > 0).sum())
        fixed = max(1, used // 4)
        moved = fixed + (places - fixed + rotation * (used - fixed)) % max(1, amount - fixed)
        return jnp.zeros((amount,), jnp.int32).at[ranking[jnp.where(places < fixed, places, moved)]].set(jnp.asarray(tallies, jnp.int32))

    tallies = jnp.where(number % 4 == 0, named(packed, number // 4), named(common, number - number // 4 - 1))
    mixed = jax.random.permutation(jax.random.fold_in(own, 3), amount)
    giver, receiver = mixed[0:amount // 2 * 2:2], mixed[1:amount // 2 * 2:2]
    margin = jnp.minimum(tallies[giver] - 1, bound - tallies[receiver]) // 2
    margin = jnp.where((giver == ranking[0]) | (receiver == ranking[0]) | (tallies[receiver] == 0), 0, jnp.maximum(margin, 0))
    moved = jax.random.randint(jax.random.fold_in(own, 4), (amount // 2,), 0, 1 << 20) % (margin + 1)
    tallies = tallies.at[giver].add(-moved).at[receiver].add(moved)
    members = jnp.searchsorted(jnp.cumsum(tallies), jnp.arange(rows * top), side="right").astype(jnp.int32)
    listing = members.reshape(top, rows).T
    listing = listing[jax.random.permutation(jax.random.fold_in(own, 1), rows)]
    rotation = jax.random.randint(jax.random.fold_in(own, 2), (rows, 1), 0, top)
    return jnp.take_along_axis(listing, (jnp.arange(top)[None, :] + rotation) % top, axis=1)


def portions_of(amount, total, limit, skew, full):
    loads = [(1 << 20) // math.isqrt(rank ** skew) + 1 for rank in range(1, amount + 1)]
    largest = limit if full else min(limit, max(-(-total // amount), total * loads[0] // sum(loads)))
    least = 1 if total - largest >= amount - 1 else 0
    given, surplus = [largest] + [least] * (amount - 1), total - largest - least * (amount - 1)
    while surplus > 0:
        free = [i for i in range(1, amount) if given[i] < largest] or [i for i in range(1, amount) if given[i] < limit]
        mass, remaining = sum([loads[i] for i in free]), surplus
        for i in free:
            addition = min(limit - given[i], max(1, remaining * loads[i] // mass), surplus)
            given[i] = given[i] + addition
            surplus = surplus - addition
    return np.array(given)


def centred(stream_key, shape, spread, reach, split=(), kind=jnp.bfloat16):
    result = jax.random.normal(stream_key, shape, jnp.float32) * spread
    if len(split) > 0:
        result = block_levels(stream_key, shape, split, -0.22, 0.18) * result
    return jnp.clip(result, min=-reach, max=reach).astype(kind)


def setup_inputs(seed: int = 0) -> dict:
    keys = jax.random.split(jax.random.key(seed), 13)
    spectra = centred(keys[0], (POINTS, D), 1.0, 6.0, ((0, 8), (1, 4)))
    spectral_filter = centred(keys[1], (2, POINTS_DEV, N_FREQ, D), 0.7, 5.0, ((2, 8), (3, 4)))
    norm_gain = jnp.clip(1.0 + 0.18 * jax.random.normal(keys[2], (D,), jnp.float32), 0.1, 1.9)
    mlp_gate = centred(keys[3], (D, FF_ENC), D ** -0.5, 0.1875, ((1, 4),))
    mlp_up = centred(keys[4], (D, FF_ENC), D ** -0.5, 0.1875, ((1, 4),))
    mlp_down = centred(keys[5], (FF_ENC, D), FF_ENC ** -0.5, 0.125, ((0, 4),))
    expert_gain = jnp.clip(1.0 + 0.18 * jax.random.normal(keys[6], (D,), jnp.float32), 0.1, 1.9)
    expert_gate = centred(keys[7], (EXPERTS, D, FFE), D ** -0.5, 0.1875, ((0, 8), (2, 4)))
    expert_up = centred(keys[8], (EXPERTS, D, FFE), D ** -0.5, 0.1875, ((0, 8), (2, 4)))
    expert_down = centred(keys[9], (EXPERTS, FFE, D), FFE ** -0.5, 0.09375, ((0, 8), (1, 4)))
    routes_keys = jax.random.split(jax.random.fold_in(keys[10], 1), POINTS // POINTS_DEV)
    routes_turns = jax.random.permutation(jax.random.fold_in(keys[10], 3), POINTS // POINTS_DEV)
    routes = jax.vmap(lambda own, number: assign_block(jax.random.fold_in(keys[10], 2), own, number, POINTS_DEV, EXPERTS, TOP, CAP, 2))(routes_keys, routes_turns).reshape((POINTS, TOP))
    combine = set_ends(jax.random.randint(keys[11], (POINTS, TOP), 1, 9), jax.random.fold_in(keys[11], 1), 1, 8).astype(jnp.int32)
    return {"spectra": spectra, "spectral_filter": spectral_filter, "norm_gain": norm_gain, "mlp_gate": mlp_gate, "mlp_up": mlp_up, "mlp_down": mlp_down, "expert_gain": expert_gain, "expert_gate": expert_gate, "expert_up": expert_up, "expert_down": expert_down, "routes": routes, "combine": combine}


EPS = 1e-06

def rms_rows(values, gain_vec):
    values = values.astype(jnp.float32)
    inverse_rms = lax.rsqrt(lax.optimization_barrier(jnp.mean(values * values, axis=-1, keepdims=True)) + EPS)
    return (values * inverse_rms * gain_vec).astype(jnp.bfloat16)

def matmul(left, right):
    return jnp.dot(left, right, preferred_element_type=jnp.float32)

def gated(normed, gate_w, up_w):
    return (jax.nn.silu(matmul(normed, gate_w)) * matmul(normed, up_w)).astype(jnp.bfloat16)

def split_down(hidden, down_proj):
    pieces = N_CHAN * N_EXPERT
    stride = hidden.shape[1] // pieces
    summed = jnp.zeros((hidden.shape[0], down_proj.shape[1]), jnp.float32)
    for block_id in range(pieces):
        product_part = matmul(hidden[:, block_id * stride:(block_id + 1) * stride], down_proj[block_id * stride:(block_id + 1) * stride])
        rounded = lax.optimization_barrier(product_part.astype(jnp.bfloat16))
        summed = summed + rounded.astype(jnp.float32)
    return summed

def reference(spectra, spectral_filter, norm_gain, mlp_gate, mlp_up, mlp_down, expert_gain, expert_gate, expert_up, expert_down, routes, combine):
    length_all = POINTS_DEV * N_FREQ
    signal = spectra.astype(jnp.float32)
    spectrum = jnp.fft.fft(signal, axis=0)
    coefs = spectral_filter.astype(jnp.float32).reshape(2, length_all, D)
    shaped = lax.complex(coefs[0], coefs[1]) * spectrum
    mixed_sum = signal + jnp.real(jnp.fft.ifft(shaped, axis=0))
    hidden = gated(rms_rows(mixed_sum.astype(jnp.bfloat16), norm_gain), mlp_gate, mlp_up)
    encoded = mixed_sum + split_down(hidden, mlp_down)
    expert_in = rms_rows(encoded.astype(jnp.bfloat16), expert_gain)
    capacity = N_FREQ * CAP
    shares = combine.astype(jnp.float32) / 8.0

    def one_expert(summed, pack):
        gate_w, up_w, down_w, expert_id = pack
        matches = routes == expert_id
        chosen = jnp.any(matches, axis=1)
        weight = lax.optimization_barrier(jnp.sum(jnp.where(matches, shares, 0.0), axis=1))
        picked = jnp.nonzero(chosen, size=capacity, fill_value=0)[0].astype(jnp.int32)
        filled = jnp.arange(capacity, dtype=jnp.int32) < jnp.sum(chosen.astype(jnp.int32))
        rows_in = expert_in[picked]
        out_rows = lax.optimization_barrier(split_down(gated(rows_in, gate_w, up_w), down_w).astype(jnp.bfloat16))
        scaled = jnp.where(filled, weight[picked], 0.0)[:, None] * out_rows.astype(jnp.float32)
        return (summed.at[picked].add(scaled), None)
    start = jnp.zeros((length_all, D), jnp.float32)
    ids = jnp.arange(EXPERTS, dtype=jnp.int32)
    summed = lax.scan(one_expert, start, (expert_gate, expert_up, expert_down, ids))[0]
    return (encoded + summed).astype(jnp.bfloat16)
```

```python
import math

import jax
import jax.numpy as jnp
from jax import lax
from jax.sharding import PartitionSpec as P

EPS = 1e-06


def tables(height, breadth, modulus, col_start):
    left = lax.broadcasted_iota(jnp.int32, (height, breadth), 0)
    right = lax.broadcasted_iota(jnp.int32, (height, breadth), 1) + col_start
    angle = (left * right % modulus).astype(jnp.float32) * (2.0 * math.pi / modulus)
    return (jnp.cos(angle), jnp.sin(angle))


def precise(left, right):
    return matmul(left.astype(jnp.bfloat16), right.astype(jnp.bfloat16))


def matmul(left, right):
    return jnp.dot(left, right, preferred_element_type=jnp.float32)


def rms_rows(values, gain_vec):
    values = values.astype(jnp.float32)
    inverse_rms = lax.rsqrt(jnp.mean(values * values, axis=-1, keepdims=True) + EPS)
    return (values * inverse_rms * gain_vec).astype(jnp.bfloat16)


def gated(normed, gate_w, up_w):
    return (jax.nn.silu(matmul(normed, gate_w)) * matmul(normed, up_w)).astype(jnp.bfloat16)


def across_slabs(values):
    return lax.all_to_all(
        values.astype(jnp.bfloat16), "freq", split_axis=0, concat_axis=0, tiled=True
    ).astype(values.dtype)


def spectral_mix(signal, filter_pair):
    slabs = lax.axis_size("freq")
    length = signal.shape[0]
    channels = signal.shape[1]
    block_rows = length // slabs
    length_all = length * slabs
    my_slab = lax.axis_index("freq")
    cos_slab, sin_slab = tables(slabs, slabs, slabs, 0)
    cos_long, sin_long = tables(length, length, length, 0)
    gathered = across_slabs(signal).reshape(slabs, block_rows * channels)
    first_re = precise(cos_slab, gathered).reshape(slabs, block_rows, channels)
    first_im = -precise(sin_slab, gathered).reshape(slabs, block_rows, channels)
    twist_cos, twist_sin = tables(slabs, block_rows, length_all, my_slab * block_rows)
    twist_cos = twist_cos[:, :, None]
    twist_sin = twist_sin[:, :, None]
    turned_re = first_re * twist_cos + first_im * twist_sin
    turned_im = first_im * twist_cos - first_re * twist_sin
    packed = jnp.stack([turned_re, turned_im], axis=2).reshape(length, 2, channels)
    columns = across_slabs(packed)
    col_re = columns[:, 0]
    col_im = columns[:, 1]
    freq_re = precise(cos_long, col_re) + precise(sin_long, col_im)
    freq_im = precise(cos_long, col_im) - precise(sin_long, col_re)
    coef_re = filter_pair[0, :, 0].astype(jnp.float32)
    coef_im = filter_pair[1, :, 0].astype(jnp.float32)
    shaped_re = coef_re * freq_re - coef_im * freq_im
    shaped_im = coef_re * freq_im + coef_im * freq_re
    back_re = precise(cos_long, shaped_re) - precise(sin_long, shaped_im)
    back_im = precise(cos_long, shaped_im) + precise(sin_long, shaped_re)
    undo_cos, undo_sin = tables(length, 1, length_all, my_slab)
    spun_re = back_re * undo_cos - back_im * undo_sin
    spun_im = back_im * undo_cos + back_re * undo_sin
    packed_back = jnp.stack([spun_re, spun_im], axis=1)
    rows_back = across_slabs(packed_back).reshape(slabs, block_rows, 2, channels)
    real_rows = rows_back[:, :, 0].reshape(slabs, block_rows * channels)
    imag_rows = rows_back[:, :, 1].reshape(slabs, block_rows * channels)
    spatial = precise(cos_slab, real_rows) - precise(sin_slab, imag_rows)
    spatial = spatial.reshape(length, channels)
    return across_slabs(spatial) / length_all


def body(
    spectra,
    spectral_filter,
    norm_gain,
    mlp_gate,
    mlp_up,
    mlp_down,
    expert_gain,
    expert_gate,
    expert_up,
    expert_down,
    routes,
    combine,
):
    signal = spectra.astype(jnp.float32)
    mixed_sum = signal + spectral_mix(signal, spectral_filter)
    full_rows = lax.all_gather(
        mixed_sum.astype(jnp.bfloat16), ("chan", "expert"), axis=1, tiled=True
    )
    hidden = gated(rms_rows(full_rows, norm_gain), mlp_gate, mlp_up)
    encoded = mixed_sum + lax.psum_scatter(
        matmul(hidden, mlp_down).astype(jnp.bfloat16),
        ("chan", "expert"),
        scatter_dimension=1,
        tiled=True,
    ).astype(jnp.float32)
    encoded_half = encoded.astype(jnp.bfloat16)
    slabs = lax.axis_size("freq")
    length = spectra.shape[0]
    capacity = min(length, 4 * length // slabs)
    slots_all = slabs * capacity
    picks = routes.reshape(-1)
    onehot = (picks[:, None] == lax.broadcasted_iota(jnp.int32, (1, slabs), 1)).astype(jnp.int32)
    order = lax.broadcasted_iota(jnp.int32, (picks.shape[0], picks.shape[0]), 0)
    before = order > lax.broadcasted_iota(jnp.int32, order.shape, 1)
    earlier = matmul(before.astype(jnp.bfloat16), onehot.astype(jnp.bfloat16))
    position = jnp.sum(earlier.astype(jnp.int32) * onehot, axis=1)
    slot_ids = picks * capacity + position
    placed = lax.broadcasted_iota(jnp.int32, (slots_all, 1), 0) == slot_ids[None, :]
    placed = placed.reshape(slots_all, length, 2)
    send_table = jnp.any(placed, axis=2).astype(jnp.bfloat16)
    shares = combine.astype(jnp.float32) / 8.0
    merge_table = jnp.sum(jnp.where(placed, shares[None], 0.0), axis=2).astype(jnp.bfloat16)
    outgoing = matmul(send_table, encoded_half).astype(jnp.bfloat16)
    arrived = lax.all_to_all(outgoing, "freq", split_axis=0, concat_axis=0, tiled=True)
    arrived = lax.all_gather(arrived, ("chan", "expert"), axis=1, tiled=True)
    expert_in = rms_rows(arrived, expert_gain)
    expert_hidden = gated(expert_in, expert_gate[0], expert_up[0])
    partial_out = matmul(expert_hidden, expert_down[0])
    expert_out = lax.psum_scatter(
        partial_out.astype(jnp.bfloat16), ("chan", "expert"), scatter_dimension=1, tiled=True
    )
    returned = lax.all_to_all(expert_out, "freq", split_axis=0, concat_axis=0, tiled=True)
    routed_sum = lax.dot_general(
        merge_table, returned, (((0,), (0,)), ((), ())), preferred_element_type=jnp.float32
    )
    return (encoded + routed_sum).astype(jnp.bfloat16)


def solution(mesh):
    placed = (
        P("freq", ("chan", "expert")),
        P(None, None, "freq", ("chan", "expert")),
        P(),
        P(None, ("chan", "expert")),
        P(None, ("chan", "expert")),
        P(("chan", "expert"), None),
        P(),
        P("freq", None, ("chan", "expert")),
        P("freq", None, ("chan", "expert")),
        P("freq", ("chan", "expert"), None),
        P("freq", None),
        P("freq", None),
    )
    return jax.shard_map(
        body, mesh=mesh, in_specs=placed, out_specs=P("freq", ("chan", "expert")), check_vma=False
    )
```

```python
import functools
import math

import jax
import jax.numpy as jnp
from jax import lax
from jax.experimental import pallas as pl
from jax.experimental.pallas import tpu as pltpu
from jax.sharding import PartitionSpec as P

EPS = 1e-06


def tables(height, breadth, modulus, col_start):
    left = lax.broadcasted_iota(jnp.int32, (height, breadth), 0)
    right = lax.broadcasted_iota(jnp.int32, (height, breadth), 1) + col_start
    angle = (left * right % modulus).astype(jnp.float32) * (2.0 * math.pi / modulus)
    return (jnp.cos(angle), jnp.sin(angle))


def precise(left, right):
    return matmul(left.astype(jnp.bfloat16), right.astype(jnp.bfloat16))


def matmul(left, right):
    return jnp.dot(left, right, preferred_element_type=jnp.float32)


def rms_rows(values, gain_vec):
    values = values.astype(jnp.float32)
    inverse_rms = lax.rsqrt(jnp.mean(values * values, axis=-1, keepdims=True) + EPS)
    return (values * inverse_rms * gain_vec).astype(jnp.bfloat16)


def gated(normed, gate_w, up_w):
    return (jax.nn.silu(matmul(normed, gate_w)) * matmul(normed, up_w)).astype(jnp.bfloat16)


def across_slabs(values):
    return lax.all_to_all(
        values.astype(jnp.bfloat16), "freq", split_axis=0, concat_axis=0, tiled=True
    ).astype(values.dtype)


def spectral_mix(signal, filter_pair):
    slabs = lax.axis_size("freq")
    length = signal.shape[0]
    channels = signal.shape[1]
    block_rows = length // slabs
    length_all = length * slabs
    my_slab = lax.axis_index("freq")
    cos_slab, sin_slab = tables(slabs, slabs, slabs, 0)
    cos_long, sin_long = tables(length, length, length, 0)
    gathered = across_slabs(signal).reshape(slabs, block_rows * channels)
    first_re = precise(cos_slab, gathered).reshape(slabs, block_rows, channels)
    first_im = -precise(sin_slab, gathered).reshape(slabs, block_rows, channels)
    twist_cos, twist_sin = tables(slabs, block_rows, length_all, my_slab * block_rows)
    twist_cos = twist_cos[:, :, None]
    twist_sin = twist_sin[:, :, None]
    turned_re = first_re * twist_cos + first_im * twist_sin
    turned_im = first_im * twist_cos - first_re * twist_sin
    packed = jnp.stack([turned_re, turned_im], axis=2).reshape(length, 2, channels)
    columns = across_slabs(packed)
    col_re = columns[:, 0]
    col_im = columns[:, 1]
    freq_re = precise(cos_long, col_re) + precise(sin_long, col_im)
    freq_im = precise(cos_long, col_im) - precise(sin_long, col_re)
    coef_re = filter_pair[0, :, 0].astype(jnp.float32)
    coef_im = filter_pair[1, :, 0].astype(jnp.float32)
    shaped_re = coef_re * freq_re - coef_im * freq_im
    shaped_im = coef_re * freq_im + coef_im * freq_re
    back_re = precise(cos_long, shaped_re) - precise(sin_long, shaped_im)
    back_im = precise(cos_long, shaped_im) + precise(sin_long, shaped_re)
    undo_cos, undo_sin = tables(length, 1, length_all, my_slab)
    spun_re = back_re * undo_cos - back_im * undo_sin
    spun_im = back_im * undo_cos + back_re * undo_sin
    packed_back = jnp.stack([spun_re, spun_im], axis=1)
    rows_back = across_slabs(packed_back).reshape(slabs, block_rows, 2, channels)
    real_rows = rows_back[:, :, 0].reshape(slabs, block_rows * channels)
    imag_rows = rows_back[:, :, 1].reshape(slabs, block_rows * channels)
    spatial = precise(cos_slab, real_rows) - precise(sin_slab, imag_rows)
    spatial = spatial.reshape(length, channels)
    return across_slabs(spatial) / length_all


def experts_kernel(
    slabs,
    per,
    out_ref_rows,
    gain_ref,
    gate_hbm,
    up_hbm,
    down_hbm,
    back_ref,
    gate_ref,
    up_ref,
    down_ref,
    rows_ref,
    normed_ref,
    hidden_ref,
    part_ref,
    pair_ref,
    turn_ref,
    cross_ref,
    final_ref,
    ret_ref,
    weight_sem,
    disp_send,
    disp_recv,
    x_send,
    x_recv,
    sib_send,
    sib_recv,
    fwd_send,
    fwd_recv,
    pair_send,
    pair_recv,
    cross_send,
    cross_recv,
    ret_send,
    ret_recv,
):
    me = lax.axis_index("freq")
    chan = lax.axis_index("chan")
    core = lax.axis_index("expert")
    mine = chan * 2 + core
    other = (1 - chan) * 2 + core
    groups = slabs // per
    capacity, width = rows_ref.shape[2], rows_ref.shape[3]
    rows = per * capacity

    loads = [
        pltpu.make_async_copy(source, target, weight_sem.at[number])
        for number, (source, target) in enumerate(
            ((gate_hbm, gate_ref), (up_hbm, up_ref), (down_hbm, down_ref))
        )
    ]
    for load in loads:
        load.start()

    barrier = pltpu.get_barrier_semaphore()
    for k in range(1, slabs):
        pl.semaphore_signal(
            barrier, inc=1, device_id={"freq": lax.rem(me + k, slabs)}, device_id_type=pl.DeviceIdType.MESH
        )
    pl.semaphore_signal(barrier, inc=1, device_id={"chan": 1 - chan}, device_id_type=pl.DeviceIdType.MESH)
    pl.semaphore_signal(barrier, inc=1, device_id={"expert": 1 - core}, device_id_type=pl.DeviceIdType.MESH)
    pl.semaphore_wait(barrier, slabs + 1)

    def remote(source, target, send, recv, device):
        return pltpu.make_async_remote_copy(
            src_ref=source,
            dst_ref=target,
            send_sem=send,
            recv_sem=recv,
            device_id=device,
            device_id_type=pl.DeviceIdType.MESH,
        )

    def dispatch(k):
        peer = lax.rem(me + k, slabs)
        return remote(
            out_ref_rows.at[peer], rows_ref.at[mine, k], disp_send.at[k], disp_recv.at[k], {"freq": peer}
        )

    def span(i):
        return pl.ds(i * per, per)

    def to_cross(i):
        block = rows_ref.at[mine, span(i)]
        return remote(block, block, x_send.at[i], x_recv.at[i], {"chan": 1 - chan})

    def from_cross(i):
        block = rows_ref.at[other, span(i)]
        return remote(block, block, x_send.at[i], x_recv.at[i], {"chan": 1 - chan})

    def to_sibling(i):
        block = rows_ref.at[mine, span(i)]
        return remote(block, block, sib_send.at[i], sib_recv.at[i], {"expert": 1 - core})

    def forward(i):
        block = rows_ref.at[other, span(i)]
        return remote(block, block, fwd_send.at[i], fwd_recv.at[i], {"expert": 1 - core})

    def pair(c, i):
        return remote(
            part_ref.at[c * 2 + 1 - core, span(i)],
            pair_ref.at[c, span(i)],
            pair_send.at[c, i],
            pair_recv.at[c, i],
            {"expert": 1 - core},
        )

    def cross(i):
        return remote(
            turn_ref.at[span(i)], cross_ref.at[span(i)], cross_send.at[i], cross_recv.at[i], {"chan": 1 - chan}
        )

    def give_back(k):
        home = lax.rem(me - k + slabs, slabs)
        return remote(final_ref.at[k], ret_ref.at[k], ret_send.at[k], ret_recv.at[k], {"freq": home})

    def arrive(i):
        for j in range(per):
            k = i * per + j

            @pl.when(k > 0)
            def _():
                dispatch(k).wait_recv()

        to_cross(i).start()
        to_sibling(i).start()

    def pass_on(i):
        from_cross(i).wait_recv()
        forward(i).start()

    def compute(i):
        to_sibling(i).wait_recv()
        forward(i).wait_recv()
        quarters = [
            rows_ref[q, span(i)].reshape(rows, width).astype(jnp.float32) for q in range(4)
        ]
        total = sum(jnp.sum(x * x, axis=-1, keepdims=True) for x in quarters)
        scale = lax.rsqrt(total / (4 * width) + EPS)
        for q in range(4):
            cols = slice(q * width, (q + 1) * width)
            normed_ref[:, cols] = (quarters[q] * scale * gain_ref[:, cols]).astype(jnp.bfloat16)

        @pl.when(i == 0)
        def _():
            for load in loads:
                load.wait()

        tile = 256
        for start in range(0, hidden_ref.shape[1], tile):
            cols = slice(start, start + tile)
            gate = matmul(normed_ref[...], gate_ref[0, :, cols])
            up = matmul(normed_ref[...], up_ref[0, :, cols])
            hidden_ref[:, cols] = (gate / (1.0 + jnp.exp(-gate)) * up).astype(jnp.bfloat16)
        for q in range(4):
            part = matmul(hidden_ref[...], down_ref[0, :, q * width : (q + 1) * width])
            part_ref[q, span(i)] = part.astype(jnp.bfloat16).reshape(per, capacity, width)
        pair(0, i).start()
        pair(1, i).start()

    def both(q, c, i):
        return part_ref[q, span(i)].astype(jnp.float32) + pair_ref[c, span(i)].astype(jnp.float32)

    def turn(i):
        pair(0, i).wait_recv()
        pair(1, i).wait_recv()
        turn_ref[span(i)] = both(other, 1 - chan, i).astype(jnp.bfloat16)
        cross(i).start()

    def finish(i):
        cross(i).wait_recv()
        final_ref[span(i)] = (both(mine, chan, i) + cross_ref[span(i)].astype(jnp.float32)).astype(
            jnp.bfloat16
        )
        for j in range(per):
            k = i * per + j

            @pl.when(k > 0)
            def _():
                give_back(k).start()

    for k in range(1, slabs):
        dispatch(k).start()
    rows_ref[mine, 0] = out_ref_rows[me]
    arrive(0)
    pass_on(0)

    def step(i, carry):
        @pl.when(i + 1 < groups)
        def _():
            arrive(i + 1)

        compute(i)

        @pl.when(i + 1 < groups)
        def _():
            pass_on(i + 1)

        @pl.when(i >= 1)
        def _():
            turn(i - 1)

        @pl.when(i >= 2)
        def _():
            finish(i - 2)

        return carry

    lax.fori_loop(0, groups, step, 0)
    turn(groups - 1)
    if groups >= 2:
        finish(groups - 2)
    finish(groups - 1)
    back_ref[me] = final_ref[0]
    for k in range(1, slabs):
        give_back(k).wait_recv()
        back_ref[lax.rem(me + k, slabs)] = ret_ref[k]
    for k in range(1, slabs):
        dispatch(k).wait_send()
        give_back(k).wait_send()
    for i in range(groups):
        to_cross(i).wait_send()
        to_sibling(i).wait_send()
        forward(i).wait_send()
        pair(0, i).wait_send()
        pair(1, i).wait_send()
        cross(i).wait_send()


def experts_direct(outgoing, gain, gate_w, up_w, down_w):
    slabs, capacity, width = outgoing.shape
    per = max(1, 256 // capacity)
    groups = slabs // per
    hidden = gate_w.shape[2]
    half = jnp.bfloat16
    dma = pltpu.SemaphoreType.DMA
    vmem = pl.BlockSpec(memory_space=pltpu.VMEM)
    hbm = pl.BlockSpec(memory_space=pl.ANY)
    return pl.pallas_call(
        functools.partial(experts_kernel, slabs, per),
        out_shape=jax.ShapeDtypeStruct(outgoing.shape, half),
        in_specs=[vmem, vmem, hbm, hbm, hbm],
        out_specs=vmem,
        scratch_shapes=[
            pltpu.VMEM(gate_w.shape, half),
            pltpu.VMEM(up_w.shape, half),
            pltpu.VMEM(down_w.shape, half),
            pltpu.VMEM((4, slabs, capacity, width), half),
            pltpu.VMEM((per * capacity, 4 * width), half),
            pltpu.VMEM((per * capacity, hidden), half),
            pltpu.VMEM((4, slabs, capacity, width), half),
            pltpu.VMEM((2, slabs, capacity, width), half),
            pltpu.VMEM((slabs, capacity, width), half),
            pltpu.VMEM((slabs, capacity, width), half),
            pltpu.VMEM((slabs, capacity, width), half),
            pltpu.VMEM((slabs, capacity, width), half),
            dma((3,)),
            dma((slabs,)),
            dma((slabs,)),
            dma((groups,)),
            dma((groups,)),
            dma((groups,)),
            dma((groups,)),
            dma((groups,)),
            dma((groups,)),
            dma((2, groups)),
            dma((2, groups)),
            dma((groups,)),
            dma((groups,)),
            dma((slabs,)),
            dma((slabs,)),
        ],
        compiler_params=pltpu.CompilerParams(
            collective_id=1, has_side_effects=True, vmem_limit_bytes=36 * 1024 * 1024
        ),
        cost_estimate=pl.CostEstimate(
            flops=6 * slabs * capacity * 4 * width * hidden, bytes_accessed=3 * 8 * width * hidden, transcendentals=0
        ),
    )(outgoing, gain[None], gate_w, up_w, down_w)


def experts_plain(outgoing, gain, gate_w, up_w, down_w):
    slabs, capacity, width = outgoing.shape
    arrived = lax.all_to_all(outgoing, "freq", split_axis=0, concat_axis=0, tiled=True)
    arrived = lax.all_gather(arrived, ("chan", "expert"), axis=2, tiled=True).reshape(slabs * capacity, -1)
    expert_hidden = gated(rms_rows(arrived, gain), gate_w[0], up_w[0])
    expert_out = lax.psum_scatter(
        matmul(expert_hidden, down_w[0]).astype(jnp.bfloat16), ("chan", "expert"), scatter_dimension=1, tiled=True
    ).reshape(slabs, capacity, width)
    return lax.all_to_all(expert_out, "freq", split_axis=0, concat_axis=0, tiled=True)


def body(
    spectra,
    spectral_filter,
    norm_gain,
    mlp_gate,
    mlp_up,
    mlp_down,
    expert_gain,
    expert_gate,
    expert_up,
    expert_down,
    routes,
    combine,
):
    signal = spectra.astype(jnp.float32)
    mixed_sum = signal + spectral_mix(signal, spectral_filter)
    full_rows = lax.all_gather(
        mixed_sum.astype(jnp.bfloat16), ("chan", "expert"), axis=1, tiled=True
    )
    hidden = gated(rms_rows(full_rows, norm_gain), mlp_gate, mlp_up)
    encoded = mixed_sum + lax.psum_scatter(
        matmul(hidden, mlp_down).astype(jnp.bfloat16),
        ("chan", "expert"),
        scatter_dimension=1,
        tiled=True,
    ).astype(jnp.float32)
    encoded_half = encoded.astype(jnp.bfloat16)
    slabs = lax.axis_size("freq")
    length = spectra.shape[0]
    capacity = min(length, 4 * length // slabs)
    slots_all = slabs * capacity
    picks = routes.reshape(-1)
    onehot = (picks[:, None] == lax.broadcasted_iota(jnp.int32, (1, slabs), 1)).astype(jnp.int32)
    order = lax.broadcasted_iota(jnp.int32, (picks.shape[0], picks.shape[0]), 0)
    before = order > lax.broadcasted_iota(jnp.int32, order.shape, 1)
    earlier = matmul(before.astype(jnp.bfloat16), onehot.astype(jnp.bfloat16))
    position = jnp.sum(earlier.astype(jnp.int32) * onehot, axis=1)
    slot_ids = picks * capacity + position
    placed = lax.broadcasted_iota(jnp.int32, (slots_all, 1), 0) == slot_ids[None, :]
    placed = placed.reshape(slots_all, length, 2)
    send_table = jnp.any(placed, axis=2).astype(jnp.bfloat16)
    shares = combine.astype(jnp.float32) / 8.0
    merge_table = jnp.sum(jnp.where(placed, shares[None], 0.0), axis=2).astype(jnp.bfloat16)
    outgoing = matmul(send_table, encoded_half).astype(jnp.bfloat16)
    outgoing = outgoing.reshape(slabs, capacity, -1)
    direct = (
        lax.axis_size("chan") == 2
        and lax.axis_size("expert") == 2
        and capacity % 16 == 0
        and slabs % max(1, 256 // capacity) == 0
    )
    experts = experts_direct if direct else experts_plain
    returned = experts(outgoing, expert_gain, expert_gate, expert_up, expert_down).reshape(slots_all, -1)
    routed_sum = lax.dot_general(
        merge_table, returned, (((0,), (0,)), ((), ())), preferred_element_type=jnp.float32
    )
    return (encoded + routed_sum).astype(jnp.bfloat16)


def solution(mesh):
    placed = (
        P("freq", ("chan", "expert")),
        P(None, None, "freq", ("chan", "expert")),
        P(),
        P(None, ("chan", "expert")),
        P(None, ("chan", "expert")),
        P(("chan", "expert"), None),
        P(),
        P("freq", None, ("chan", "expert")),
        P("freq", None, ("chan", "expert")),
        P("freq", ("chan", "expert"), None),
        P("freq", None),
        P("freq", None),
    )
    return jax.shard_map(
        body, mesh=mesh, in_specs=placed, out_specs=P("freq", ("chan", "expert")), check_vma=False
    )
```

```python
import functools
import math

import jax
import jax.numpy as jnp
from jax import lax
from jax.experimental import pallas as pl
from jax.experimental.pallas import tpu as pltpu
from jax.sharding import PartitionSpec as P

EPS = 1e-06


def tables(height, breadth, modulus, col_start):
    left = lax.broadcasted_iota(jnp.int32, (height, breadth), 0)
    right = lax.broadcasted_iota(jnp.int32, (height, breadth), 1) + col_start
    angle = (left * right % modulus).astype(jnp.float32) * (2.0 * math.pi / modulus)
    return (jnp.cos(angle), jnp.sin(angle))


def precise(left, right):
    return matmul(left.astype(jnp.bfloat16), right.astype(jnp.bfloat16))


def matmul(left, right):
    return jnp.dot(left, right, preferred_element_type=jnp.float32)


def rms_rows(values, gain_vec):
    values = values.astype(jnp.float32)
    inverse_rms = lax.rsqrt(jnp.mean(values * values, axis=-1, keepdims=True) + EPS)
    return (values * inverse_rms * gain_vec).astype(jnp.bfloat16)


def gated(normed, gate_w, up_w):
    return (jax.nn.silu(matmul(normed, gate_w)) * matmul(normed, up_w)).astype(jnp.bfloat16)


def exchange_kernel(slabs, src_ref, dst_ref, land_ref, send_sem, recv_sem):
    me = lax.axis_index("freq")
    barrier = pltpu.get_barrier_semaphore()
    for k in range(1, slabs):
        pl.semaphore_signal(
            barrier, inc=1, device_id={"freq": lax.rem(me + k, slabs)}, device_id_type=pl.DeviceIdType.MESH
        )
    pl.semaphore_wait(barrier, slabs - 1)
    copies = []
    for k in range(1, slabs):
        peer = lax.rem(me + k, slabs)
        copy = pltpu.make_async_remote_copy(
            src_ref=src_ref.at[peer],
            dst_ref=land_ref.at[k],
            send_sem=send_sem.at[k],
            recv_sem=recv_sem.at[k],
            device_id={"freq": peer},
            device_id_type=pl.DeviceIdType.MESH,
        )
        copy.start()
        copies.append(copy)
    dst_ref[me] = src_ref[me]
    for k in range(1, slabs):
        copies[k - 1].wait_recv()
        dst_ref[lax.rem(me - k + slabs, slabs)] = land_ref[k]
    for copy in copies:
        copy.wait_send()


def across_slabs(values, number):
    slabs = values.shape[0]
    values = values.astype(jnp.bfloat16)
    if values.shape[1] % 16:
        return lax.all_to_all(values, "freq", split_axis=0, concat_axis=0, tiled=True)
    vmem = pl.BlockSpec(memory_space=pltpu.VMEM)
    return pl.pallas_call(
        functools.partial(exchange_kernel, slabs),
        out_shape=jax.ShapeDtypeStruct(values.shape, jnp.bfloat16),
        in_specs=[vmem],
        out_specs=vmem,
        scratch_shapes=[
            pltpu.VMEM(values.shape, jnp.bfloat16),
            pltpu.SemaphoreType.DMA((slabs,)),
            pltpu.SemaphoreType.DMA((slabs,)),
        ],
        compiler_params=pltpu.CompilerParams(collective_id=number, has_side_effects=True),
    )(values)


def spectral_mix(signal, filter_pair):
    slabs = lax.axis_size("freq")
    length = signal.shape[0]
    channels = signal.shape[1]
    block_rows = length // slabs
    length_all = length * slabs
    my_slab = lax.axis_index("freq")
    cos_slab, sin_slab = tables(slabs, slabs, slabs, 0)
    cos_long, sin_long = tables(length, length, length, 0)
    gathered = across_slabs(signal.reshape(slabs, block_rows, channels), 2).reshape(
        slabs, block_rows * channels
    )
    first_re = precise(cos_slab, gathered).reshape(slabs, block_rows, channels)
    first_im = -precise(sin_slab, gathered).reshape(slabs, block_rows, channels)
    twist_cos, twist_sin = tables(slabs, block_rows, length_all, my_slab * block_rows)
    twist_cos = twist_cos[:, :, None]
    twist_sin = twist_sin[:, :, None]
    turned_re = first_re * twist_cos + first_im * twist_sin
    turned_im = first_im * twist_cos - first_re * twist_sin
    packed = jnp.concatenate([turned_re, turned_im], axis=1)
    columns = across_slabs(packed, 3)
    col_re = columns[:, :block_rows].reshape(length, channels)
    col_im = columns[:, block_rows:].reshape(length, channels)
    freq_re = precise(cos_long, col_re) + precise(sin_long, col_im)
    freq_im = precise(cos_long, col_im) - precise(sin_long, col_re)
    coef_re = filter_pair[0, :, 0].astype(jnp.float32)
    coef_im = filter_pair[1, :, 0].astype(jnp.float32)
    shaped_re = coef_re * freq_re - coef_im * freq_im
    shaped_im = coef_re * freq_im + coef_im * freq_re
    back_re = precise(cos_long, shaped_re) - precise(sin_long, shaped_im)
    back_im = precise(cos_long, shaped_im) + precise(sin_long, shaped_re)
    undo_cos, undo_sin = tables(length, 1, length_all, my_slab)
    spun_re = back_re * undo_cos - back_im * undo_sin
    spun_im = back_im * undo_cos + back_re * undo_sin
    shape = (slabs, block_rows, channels)
    packed_back = jnp.concatenate([spun_re.reshape(shape), spun_im.reshape(shape)], axis=1)
    rows_back = across_slabs(packed_back, 4)
    real_rows = rows_back[:, :block_rows].reshape(slabs, block_rows * channels)
    imag_rows = rows_back[:, block_rows:].reshape(slabs, block_rows * channels)
    spatial = precise(cos_slab, real_rows) - precise(sin_slab, imag_rows)
    spatial = across_slabs(spatial.reshape(shape), 5).reshape(length, channels)
    return spatial.astype(jnp.float32) / length_all


def experts_kernel(
    slabs,
    per,
    out_ref_rows,
    gain_ref,
    gate_hbm,
    up_hbm,
    down_hbm,
    back_ref,
    gate_ref,
    up_ref,
    down_ref,
    rows_ref,
    normed_ref,
    hidden_ref,
    part_ref,
    pair_ref,
    turn_ref,
    cross_ref,
    final_ref,
    ret_ref,
    weight_sem,
    disp_send,
    disp_recv,
    x_send,
    x_recv,
    sib_send,
    sib_recv,
    fwd_send,
    fwd_recv,
    pair_send,
    pair_recv,
    cross_send,
    cross_recv,
    ret_send,
    ret_recv,
):
    me = lax.axis_index("freq")
    chan = lax.axis_index("chan")
    core = lax.axis_index("expert")
    mine = chan * 2 + core
    other = (1 - chan) * 2 + core
    groups = slabs // per
    capacity, width = rows_ref.shape[2], rows_ref.shape[3]
    rows = per * capacity

    loads = [
        pltpu.make_async_copy(source, target, weight_sem.at[number])
        for number, (source, target) in enumerate(
            ((gate_hbm, gate_ref), (up_hbm, up_ref), (down_hbm, down_ref))
        )
    ]
    for load in loads:
        load.start()

    barrier = pltpu.get_barrier_semaphore()
    for k in range(1, slabs):
        pl.semaphore_signal(
            barrier, inc=1, device_id={"freq": lax.rem(me + k, slabs)}, device_id_type=pl.DeviceIdType.MESH
        )
    pl.semaphore_signal(barrier, inc=1, device_id={"chan": 1 - chan}, device_id_type=pl.DeviceIdType.MESH)
    pl.semaphore_signal(barrier, inc=1, device_id={"expert": 1 - core}, device_id_type=pl.DeviceIdType.MESH)
    pl.semaphore_wait(barrier, slabs + 1)

    def remote(source, target, send, recv, device):
        return pltpu.make_async_remote_copy(
            src_ref=source,
            dst_ref=target,
            send_sem=send,
            recv_sem=recv,
            device_id=device,
            device_id_type=pl.DeviceIdType.MESH,
        )

    def dispatch(k):
        peer = lax.rem(me + k, slabs)
        return remote(
            out_ref_rows.at[peer], rows_ref.at[mine, k], disp_send.at[k], disp_recv.at[k], {"freq": peer}
        )

    def span(i):
        return pl.ds(i * per, per)

    def to_cross(i):
        block = rows_ref.at[mine, span(i)]
        return remote(block, block, x_send.at[i], x_recv.at[i], {"chan": 1 - chan})

    def from_cross(i):
        block = rows_ref.at[other, span(i)]
        return remote(block, block, x_send.at[i], x_recv.at[i], {"chan": 1 - chan})

    def to_sibling(i):
        block = rows_ref.at[mine, span(i)]
        return remote(block, block, sib_send.at[i], sib_recv.at[i], {"expert": 1 - core})

    def forward(i):
        block = rows_ref.at[other, span(i)]
        return remote(block, block, fwd_send.at[i], fwd_recv.at[i], {"expert": 1 - core})

    def pair(c, i):
        return remote(
            part_ref.at[c * 2 + 1 - core, span(i)],
            pair_ref.at[c, span(i)],
            pair_send.at[c, i],
            pair_recv.at[c, i],
            {"expert": 1 - core},
        )

    def cross(i):
        return remote(
            turn_ref.at[span(i)], cross_ref.at[span(i)], cross_send.at[i], cross_recv.at[i], {"chan": 1 - chan}
        )

    def give_back(k):
        home = lax.rem(me - k + slabs, slabs)
        return remote(final_ref.at[k], ret_ref.at[k], ret_send.at[k], ret_recv.at[k], {"freq": home})

    def arrive(i):
        for j in range(per):
            k = i * per + j

            @pl.when(k > 0)
            def _():
                dispatch(k).wait_recv()

        to_cross(i).start()
        to_sibling(i).start()

    def pass_on(i):
        from_cross(i).wait_recv()
        forward(i).start()

    def compute(i):
        to_sibling(i).wait_recv()
        forward(i).wait_recv()
        quarters = [
            rows_ref[q, span(i)].reshape(rows, width).astype(jnp.float32) for q in range(4)
        ]
        total = sum(jnp.sum(x * x, axis=-1, keepdims=True) for x in quarters)
        scale = lax.rsqrt(total / (4 * width) + EPS)
        for q in range(4):
            cols = slice(q * width, (q + 1) * width)
            normed_ref[:, cols] = (quarters[q] * scale * gain_ref[:, cols]).astype(jnp.bfloat16)

        @pl.when(i == 0)
        def _():
            for load in loads:
                load.wait()

        tile = 256
        for start in range(0, hidden_ref.shape[1], tile):
            cols = slice(start, start + tile)
            gate = matmul(normed_ref[...], gate_ref[0, :, cols])
            up = matmul(normed_ref[...], up_ref[0, :, cols])
            hidden_ref[:, cols] = (gate / (1.0 + jnp.exp(-gate)) * up).astype(jnp.bfloat16)
        for q in range(4):
            part = matmul(hidden_ref[...], down_ref[0, :, q * width : (q + 1) * width])
            part_ref[q, span(i)] = part.astype(jnp.bfloat16).reshape(per, capacity, width)
        pair(0, i).start()
        pair(1, i).start()

    def both(q, c, i):
        return part_ref[q, span(i)].astype(jnp.float32) + pair_ref[c, span(i)].astype(jnp.float32)

    def turn(i):
        pair(0, i).wait_recv()
        pair(1, i).wait_recv()
        turn_ref[span(i)] = both(other, 1 - chan, i).astype(jnp.bfloat16)
        cross(i).start()

    def finish(i):
        cross(i).wait_recv()
        final_ref[span(i)] = (both(mine, chan, i) + cross_ref[span(i)].astype(jnp.float32)).astype(
            jnp.bfloat16
        )
        for j in range(per):
            k = i * per + j

            @pl.when(k > 0)
            def _():
                give_back(k).start()

    for k in range(1, slabs):
        dispatch(k).start()
    rows_ref[mine, 0] = out_ref_rows[me]
    arrive(0)
    pass_on(0)

    def step(i, carry):
        @pl.when(i + 1 < groups)
        def _():
            arrive(i + 1)

        compute(i)

        @pl.when(i + 1 < groups)
        def _():
            pass_on(i + 1)

        @pl.when(i >= 1)
        def _():
            turn(i - 1)

        @pl.when(i >= 2)
        def _():
            finish(i - 2)

        return carry

    lax.fori_loop(0, groups, step, 0)
    turn(groups - 1)
    if groups >= 2:
        finish(groups - 2)
    finish(groups - 1)
    back_ref[me] = final_ref[0]
    for k in range(1, slabs):
        give_back(k).wait_recv()
        back_ref[lax.rem(me + k, slabs)] = ret_ref[k]
    for k in range(1, slabs):
        dispatch(k).wait_send()
        give_back(k).wait_send()
    for i in range(groups):
        to_cross(i).wait_send()
        to_sibling(i).wait_send()
        forward(i).wait_send()
        pair(0, i).wait_send()
        pair(1, i).wait_send()
        cross(i).wait_send()


def experts_direct(outgoing, gain, gate_w, up_w, down_w):
    slabs, capacity, width = outgoing.shape
    per = max(1, 256 // capacity)
    groups = slabs // per
    hidden = gate_w.shape[2]
    half = jnp.bfloat16
    dma = pltpu.SemaphoreType.DMA
    vmem = pl.BlockSpec(memory_space=pltpu.VMEM)
    hbm = pl.BlockSpec(memory_space=pl.ANY)
    return pl.pallas_call(
        functools.partial(experts_kernel, slabs, per),
        out_shape=jax.ShapeDtypeStruct(outgoing.shape, half),
        in_specs=[vmem, vmem, hbm, hbm, hbm],
        out_specs=vmem,
        scratch_shapes=[
            pltpu.VMEM(gate_w.shape, half),
            pltpu.VMEM(up_w.shape, half),
            pltpu.VMEM(down_w.shape, half),
            pltpu.VMEM((4, slabs, capacity, width), half),
            pltpu.VMEM((per * capacity, 4 * width), half),
            pltpu.VMEM((per * capacity, hidden), half),
            pltpu.VMEM((4, slabs, capacity, width), half),
            pltpu.VMEM((2, slabs, capacity, width), half),
            pltpu.VMEM((slabs, capacity, width), half),
            pltpu.VMEM((slabs, capacity, width), half),
            pltpu.VMEM((slabs, capacity, width), half),
            pltpu.VMEM((slabs, capacity, width), half),
            dma((3,)),
            dma((slabs,)),
            dma((slabs,)),
            dma((groups,)),
            dma((groups,)),
            dma((groups,)),
            dma((groups,)),
            dma((groups,)),
            dma((groups,)),
            dma((2, groups)),
            dma((2, groups)),
            dma((groups,)),
            dma((groups,)),
            dma((slabs,)),
            dma((slabs,)),
        ],
        compiler_params=pltpu.CompilerParams(
            collective_id=1, has_side_effects=True, vmem_limit_bytes=36 * 1024 * 1024
        ),
        cost_estimate=pl.CostEstimate(
            flops=6 * slabs * capacity * 4 * width * hidden, bytes_accessed=3 * 8 * width * hidden, transcendentals=0
        ),
    )(outgoing, gain[None], gate_w, up_w, down_w)


def experts_plain(outgoing, gain, gate_w, up_w, down_w):
    slabs, capacity, width = outgoing.shape
    arrived = lax.all_to_all(outgoing, "freq", split_axis=0, concat_axis=0, tiled=True)
    arrived = lax.all_gather(arrived, ("chan", "expert"), axis=2, tiled=True).reshape(slabs * capacity, -1)
    expert_hidden = gated(rms_rows(arrived, gain), gate_w[0], up_w[0])
    expert_out = lax.psum_scatter(
        matmul(expert_hidden, down_w[0]).astype(jnp.bfloat16), ("chan", "expert"), scatter_dimension=1, tiled=True
    ).reshape(slabs, capacity, width)
    return lax.all_to_all(expert_out, "freq", split_axis=0, concat_axis=0, tiled=True)


def body(
    spectra,
    spectral_filter,
    norm_gain,
    mlp_gate,
    mlp_up,
    mlp_down,
    expert_gain,
    expert_gate,
    expert_up,
    expert_down,
    routes,
    combine,
):
    signal = spectra.astype(jnp.float32)
    mixed_sum = signal + spectral_mix(signal, spectral_filter)
    full_rows = lax.all_gather(
        mixed_sum.astype(jnp.bfloat16), ("chan", "expert"), axis=1, tiled=True
    )
    hidden = gated(rms_rows(full_rows, norm_gain), mlp_gate, mlp_up)
    encoded = mixed_sum + lax.psum_scatter(
        matmul(hidden, mlp_down).astype(jnp.bfloat16),
        ("chan", "expert"),
        scatter_dimension=1,
        tiled=True,
    ).astype(jnp.float32)
    encoded_half = encoded.astype(jnp.bfloat16)
    slabs = lax.axis_size("freq")
    length = spectra.shape[0]
    capacity = min(length, 4 * length // slabs)
    slots_all = slabs * capacity
    picks = routes.reshape(-1)
    onehot = (picks[:, None] == lax.broadcasted_iota(jnp.int32, (1, slabs), 1)).astype(jnp.int32)
    order = lax.broadcasted_iota(jnp.int32, (picks.shape[0], picks.shape[0]), 0)
    before = order > lax.broadcasted_iota(jnp.int32, order.shape, 1)
    earlier = matmul(before.astype(jnp.bfloat16), onehot.astype(jnp.bfloat16))
    position = jnp.sum(earlier.astype(jnp.int32) * onehot, axis=1)
    slot_ids = picks * capacity + position
    placed = lax.broadcasted_iota(jnp.int32, (slots_all, 1), 0) == slot_ids[None, :]
    placed = placed.reshape(slots_all, length, 2)
    send_table = jnp.any(placed, axis=2).astype(jnp.bfloat16)
    shares = combine.astype(jnp.float32) / 8.0
    merge_table = jnp.sum(jnp.where(placed, shares[None], 0.0), axis=2).astype(jnp.bfloat16)
    outgoing = matmul(send_table, encoded_half).astype(jnp.bfloat16)
    outgoing = outgoing.reshape(slabs, capacity, -1)
    direct = (
        lax.axis_size("chan") == 2
        and lax.axis_size("expert") == 2
        and capacity % 16 == 0
        and slabs % max(1, 256 // capacity) == 0
    )
    experts = experts_direct if direct else experts_plain
    returned = experts(outgoing, expert_gain, expert_gate, expert_up, expert_down).reshape(slots_all, -1)
    routed_sum = lax.dot_general(
        merge_table, returned, (((0,), (0,)), ((), ())), preferred_element_type=jnp.float32
    )
    return (encoded + routed_sum).astype(jnp.bfloat16)


def solution(mesh):
    placed = (
        P("freq", ("chan", "expert")),
        P(None, None, "freq", ("chan", "expert")),
        P(),
        P(None, ("chan", "expert")),
        P(None, ("chan", "expert")),
        P(("chan", "expert"), None),
        P(),
        P("freq", None, ("chan", "expert")),
        P("freq", None, ("chan", "expert")),
        P("freq", ("chan", "expert"), None),
        P("freq", None),
        P("freq", None),
    )
    return jax.shard_map(
        body, mesh=mesh, in_specs=placed, out_specs=P("freq", ("chan", "expert")), check_vma=False
    )
```

```python
import functools
import math

import jax
import jax.numpy as jnp
from jax import lax
from jax.experimental import pallas as pl
from jax.experimental.pallas import tpu as pltpu
from jax.sharding import PartitionSpec as P

EPS = 1e-06


def tables(height, breadth, modulus, col_start):
    left = lax.broadcasted_iota(jnp.int32, (height, breadth), 0)
    right = lax.broadcasted_iota(jnp.int32, (height, breadth), 1) + col_start
    angle = (left * right % modulus).astype(jnp.float32) * (2.0 * math.pi / modulus)
    return (jnp.cos(angle), jnp.sin(angle))


def precise(left, right):
    return matmul(left.astype(jnp.bfloat16), right.astype(jnp.bfloat16))


def matmul(left, right):
    return jnp.dot(left, right, preferred_element_type=jnp.float32)


def rms_rows(values, gain_vec):
    values = values.astype(jnp.float32)
    inverse_rms = lax.rsqrt(jnp.mean(values * values, axis=-1, keepdims=True) + EPS)
    return (values * inverse_rms * gain_vec).astype(jnp.bfloat16)


def gated(normed, gate_w, up_w):
    return (jax.nn.silu(matmul(normed, gate_w)) * matmul(normed, up_w)).astype(jnp.bfloat16)


def across_slabs(values):
    return lax.all_to_all(
        values.astype(jnp.bfloat16), "freq", split_axis=0, concat_axis=0, tiled=True
    ).astype(values.dtype)


def spectral_mix(signal, filter_pair):
    slabs = lax.axis_size("freq")
    length = signal.shape[0]
    channels = signal.shape[1]
    block_rows = length // slabs
    length_all = length * slabs
    my_slab = lax.axis_index("freq")
    cos_slab, sin_slab = tables(slabs, slabs, slabs, 0)
    cos_long, sin_long = tables(length, length, length, 0)
    gathered = across_slabs(signal).reshape(slabs, block_rows * channels)
    first_re = precise(cos_slab, gathered).reshape(slabs, block_rows, channels)
    first_im = -precise(sin_slab, gathered).reshape(slabs, block_rows, channels)
    twist_cos, twist_sin = tables(slabs, block_rows, length_all, my_slab * block_rows)
    twist_cos = twist_cos[:, :, None]
    twist_sin = twist_sin[:, :, None]
    turned_re = first_re * twist_cos + first_im * twist_sin
    turned_im = first_im * twist_cos - first_re * twist_sin
    packed = jnp.stack([turned_re, turned_im], axis=2).reshape(length, 2, channels)
    columns = across_slabs(packed)
    col_re = columns[:, 0]
    col_im = columns[:, 1]
    freq_re = precise(cos_long, col_re) + precise(sin_long, col_im)
    freq_im = precise(cos_long, col_im) - precise(sin_long, col_re)
    coef_re = filter_pair[0, :, 0].astype(jnp.float32)
    coef_im = filter_pair[1, :, 0].astype(jnp.float32)
    shaped_re = coef_re * freq_re - coef_im * freq_im
    shaped_im = coef_re * freq_im + coef_im * freq_re
    back_re = precise(cos_long, shaped_re) - precise(sin_long, shaped_im)
    back_im = precise(cos_long, shaped_im) + precise(sin_long, shaped_re)
    undo_cos, undo_sin = tables(length, 1, length_all, my_slab)
    spun_re = back_re * undo_cos - back_im * undo_sin
    spun_im = back_im * undo_cos + back_re * undo_sin
    packed_back = jnp.stack([spun_re, spun_im], axis=1)
    rows_back = across_slabs(packed_back).reshape(slabs, block_rows, 2, channels)
    real_rows = rows_back[:, :, 0].reshape(slabs, block_rows * channels)
    imag_rows = rows_back[:, :, 1].reshape(slabs, block_rows * channels)
    spatial = precise(cos_slab, real_rows) - precise(sin_slab, imag_rows)
    spatial = spatial.reshape(length, channels)
    return across_slabs(spatial) / length_all


def experts_kernel(
    slabs,
    per,
    out_ref_rows,
    gain_ref,
    gate_hbm,
    up_hbm,
    down_hbm,
    back_ref,
    gate_ref,
    up_ref,
    down_ref,
    rows_ref,
    normed_ref,
    hidden_ref,
    part_ref,
    pair_ref,
    turn_ref,
    cross_ref,
    final_ref,
    ret_ref,
    weight_sem,
    disp_send,
    disp_recv,
    x_send,
    x_recv,
    sib_send,
    sib_recv,
    fwd_send,
    fwd_recv,
    pair_send,
    pair_recv,
    cross_send,
    cross_recv,
    ret_send,
    ret_recv,
):
    me = lax.axis_index("freq")
    chan = lax.axis_index("chan")
    core = lax.axis_index("expert")
    mine = chan * 2 + core
    other = (1 - chan) * 2 + core
    groups = slabs // per
    capacity, width = rows_ref.shape[2], rows_ref.shape[3]
    rows = per * capacity

    loads = [
        pltpu.make_async_copy(source, target, weight_sem.at[number])
        for number, (source, target) in enumerate(
            ((gate_hbm, gate_ref), (up_hbm, up_ref), (down_hbm, down_ref))
        )
    ]
    for load in loads:
        load.start()

    barrier = pltpu.get_barrier_semaphore()
    for k in range(1, slabs):
        pl.semaphore_signal(
            barrier, inc=1, device_id={"freq": lax.rem(me + k, slabs)}, device_id_type=pl.DeviceIdType.MESH
        )
    pl.semaphore_signal(barrier, inc=1, device_id={"chan": 1 - chan}, device_id_type=pl.DeviceIdType.MESH)
    pl.semaphore_signal(barrier, inc=1, device_id={"expert": 1 - core}, device_id_type=pl.DeviceIdType.MESH)
    pl.semaphore_wait(barrier, slabs + 1)

    def remote(source, target, send, recv, device):
        return pltpu.make_async_remote_copy(
            src_ref=source,
            dst_ref=target,
            send_sem=send,
            recv_sem=recv,
            device_id=device,
            device_id_type=pl.DeviceIdType.MESH,
        )

    def dispatch(k):
        peer = lax.rem(me + k, slabs)
        return remote(
            out_ref_rows.at[peer], rows_ref.at[mine, k], disp_send.at[k], disp_recv.at[k], {"freq": peer}
        )

    def span(i):
        return pl.ds(i * per, per)

    def to_cross(i):
        block = rows_ref.at[mine, span(i)]
        return remote(block, block, x_send.at[i], x_recv.at[i], {"chan": 1 - chan})

    def from_cross(i):
        block = rows_ref.at[other, span(i)]
        return remote(block, block, x_send.at[i], x_recv.at[i], {"chan": 1 - chan})

    def to_sibling(i):
        block = rows_ref.at[mine, span(i)]
        return remote(block, block, sib_send.at[i], sib_recv.at[i], {"expert": 1 - core})

    def forward(i):
        block = rows_ref.at[other, span(i)]
        return remote(block, block, fwd_send.at[i], fwd_recv.at[i], {"expert": 1 - core})

    def pair(c, i):
        return remote(
            part_ref.at[c * 2 + 1 - core, span(i)],
            pair_ref.at[c, span(i)],
            pair_send.at[c, i],
            pair_recv.at[c, i],
            {"expert": 1 - core},
        )

    def cross(i):
        return remote(
            turn_ref.at[span(i)], cross_ref.at[span(i)], cross_send.at[i], cross_recv.at[i], {"chan": 1 - chan}
        )

    def give_back(k):
        home = lax.rem(me - k + slabs, slabs)
        return remote(final_ref.at[k], ret_ref.at[k], ret_send.at[k], ret_recv.at[k], {"freq": home})

    def arrive(i):
        for j in range(per):
            k = i * per + j

            @pl.when(k > 0)
            def _():
                dispatch(k).wait_recv()

        to_cross(i).start()
        to_sibling(i).start()

    def pass_on(i):
        from_cross(i).wait_recv()
        forward(i).start()

    def compute(i):
        to_sibling(i).wait_recv()
        forward(i).wait_recv()
        quarters = [
            rows_ref[q, span(i)].reshape(rows, width).astype(jnp.float32) for q in range(4)
        ]
        total = sum(jnp.sum(x * x, axis=-1, keepdims=True) for x in quarters)
        scale = lax.rsqrt(total / (4 * width) + EPS)
        for q in range(4):
            cols = slice(q * width, (q + 1) * width)
            normed_ref[:, cols] = (quarters[q] * scale * gain_ref[:, cols]).astype(jnp.bfloat16)

        @pl.when(i == 0)
        def _():
            for load in loads:
                load.wait()

        tile = 256
        for start in range(0, hidden_ref.shape[1], tile):
            cols = slice(start, start + tile)
            gate = matmul(normed_ref[...], gate_ref[0, :, cols])
            up = matmul(normed_ref[...], up_ref[0, :, cols])
            hidden_ref[:, cols] = (gate / (1.0 + jnp.exp(-gate)) * up).astype(jnp.bfloat16)
        for q in range(4):
            part = matmul(hidden_ref[...], down_ref[0, :, q * width : (q + 1) * width])
            part_ref[q, span(i)] = part.astype(jnp.bfloat16).reshape(per, capacity, width)
        pair(0, i).start()
        pair(1, i).start()

    def both(q, c, i):
        return part_ref[q, span(i)].astype(jnp.float32) + pair_ref[c, span(i)].astype(jnp.float32)

    def turn(i):
        pair(0, i).wait_recv()
        pair(1, i).wait_recv()
        turn_ref[span(i)] = both(other, 1 - chan, i).astype(jnp.bfloat16)
        cross(i).start()

    def finish(i):
        cross(i).wait_recv()
        final_ref[span(i)] = (both(mine, chan, i) + cross_ref[span(i)].astype(jnp.float32)).astype(
            jnp.bfloat16
        )
        for j in range(per):
            k = i * per + j

            @pl.when(k > 0)
            def _():
                give_back(k).start()

    for k in range(1, slabs):
        dispatch(k).start()
    rows_ref[mine, 0] = out_ref_rows[me]
    arrive(0)
    pass_on(0)

    def step(i, carry):
        @pl.when(i + 1 < groups)
        def _():
            arrive(i + 1)

        compute(i)

        @pl.when(i + 1 < groups)
        def _():
            pass_on(i + 1)

        @pl.when(i >= 1)
        def _():
            turn(i - 1)

        @pl.when(i >= 2)
        def _():
            finish(i - 2)

        return carry

    lax.fori_loop(0, groups, step, 0)
    turn(groups - 1)
    if groups >= 2:
        finish(groups - 2)
    finish(groups - 1)
    back_ref[me] = final_ref[0]
    for k in range(1, slabs):
        give_back(k).wait_recv()
        back_ref[lax.rem(me + k, slabs)] = ret_ref[k]
    for k in range(1, slabs):
        dispatch(k).wait_send()
        give_back(k).wait_send()
    for i in range(groups):
        to_cross(i).wait_send()
        to_sibling(i).wait_send()
        forward(i).wait_send()
        pair(0, i).wait_send()
        pair(1, i).wait_send()
        cross(i).wait_send()


def experts_direct(outgoing, gain, gate_w, up_w, down_w):
    slabs, capacity, width = outgoing.shape
    per = max(1, 256 // capacity)
    groups = slabs // per
    hidden = gate_w.shape[2]
    half = jnp.bfloat16
    dma = pltpu.SemaphoreType.DMA
    vmem = pl.BlockSpec(memory_space=pltpu.VMEM)
    hbm = pl.BlockSpec(memory_space=pl.ANY)
    return pl.pallas_call(
        functools.partial(experts_kernel, slabs, per),
        out_shape=jax.ShapeDtypeStruct(outgoing.shape, half),
        in_specs=[vmem, vmem, hbm, hbm, hbm],
        out_specs=vmem,
        scratch_shapes=[
            pltpu.VMEM(gate_w.shape, half),
            pltpu.VMEM(up_w.shape, half),
            pltpu.VMEM(down_w.shape, half),
            pltpu.VMEM((4, slabs, capacity, width), half),
            pltpu.VMEM((per * capacity, 4 * width), half),
            pltpu.VMEM((per * capacity, hidden), half),
            pltpu.VMEM((4, slabs, capacity, width), half),
            pltpu.VMEM((2, slabs, capacity, width), half),
            pltpu.VMEM((slabs, capacity, width), half),
            pltpu.VMEM((slabs, capacity, width), half),
            pltpu.VMEM((slabs, capacity, width), half),
            pltpu.VMEM((slabs, capacity, width), half),
            dma((3,)),
            dma((slabs,)),
            dma((slabs,)),
            dma((groups,)),
            dma((groups,)),
            dma((groups,)),
            dma((groups,)),
            dma((groups,)),
            dma((groups,)),
            dma((2, groups)),
            dma((2, groups)),
            dma((groups,)),
            dma((groups,)),
            dma((slabs,)),
            dma((slabs,)),
        ],
        compiler_params=pltpu.CompilerParams(
            collective_id=1, has_side_effects=True, vmem_limit_bytes=36 * 1024 * 1024
        ),
        cost_estimate=pl.CostEstimate(
            flops=6 * slabs * capacity * 4 * width * hidden, bytes_accessed=3 * 8 * width * hidden, transcendentals=0
        ),
    )(outgoing, gain[None], gate_w, up_w, down_w)


def experts_plain(outgoing, gain, gate_w, up_w, down_w):
    slabs, capacity, width = outgoing.shape
    arrived = lax.all_to_all(outgoing, "freq", split_axis=0, concat_axis=0, tiled=True)
    arrived = lax.all_gather(arrived, ("chan", "expert"), axis=2, tiled=True).reshape(slabs * capacity, -1)
    expert_hidden = gated(rms_rows(arrived, gain), gate_w[0], up_w[0])
    expert_out = lax.psum_scatter(
        matmul(expert_hidden, down_w[0]).astype(jnp.bfloat16), ("chan", "expert"), scatter_dimension=1, tiled=True
    ).reshape(slabs, capacity, width)
    return lax.all_to_all(expert_out, "freq", split_axis=0, concat_axis=0, tiled=True)


def encode_kernel(
    slabs,
    src_ref,
    filter_ref,
    cos_ref,
    sin_ref,
    twist_ref,
    undo_ref,
    gain_ref,
    gate_hbm,
    up_hbm,
    down_hbm,
    out_ref,
    gate_ref,
    up_ref,
    down_ref,
    land1,
    pack2,
    land2,
    cols_ref,
    pack3,
    land3,
    pack4,
    land4,
    mixed_ref,
    rows_ref,
    normed_ref,
    part_ref,
    pair_ref,
    turn_ref,
    cross_ref,
    weight_sem,
    swap_send,
    swap_recv,
    side_send,
    side_recv,
):
    me = lax.axis_index("freq")
    chan = lax.axis_index("chan")
    core = lax.axis_index("expert")
    mine = chan * 2 + core
    other = (1 - chan) * 2 + core
    block, width = src_ref.shape[1], src_ref.shape[2]
    length = slabs * block
    half = jnp.bfloat16
    loads = [
        pltpu.make_async_copy(source, target, weight_sem.at[number])
        for number, (source, target) in enumerate(
            ((gate_hbm, gate_ref), (up_hbm, up_ref), (down_hbm, down_ref))
        )
    ]
    for load in loads:
        load.start()
    barrier = pltpu.get_barrier_semaphore()
    for k in range(1, slabs):
        pl.semaphore_signal(
            barrier, inc=1, device_id={"freq": lax.rem(me + k, slabs)}, device_id_type=pl.DeviceIdType.MESH
        )
    pl.semaphore_signal(barrier, inc=1, device_id={"chan": 1 - chan}, device_id_type=pl.DeviceIdType.MESH)
    pl.semaphore_signal(barrier, inc=1, device_id={"expert": 1 - core}, device_id_type=pl.DeviceIdType.MESH)
    pl.semaphore_wait(barrier, slabs + 1)
    sent = []

    def remote(source, target, send, recv, device):
        copy = pltpu.make_async_remote_copy(
            src_ref=source,
            dst_ref=target,
            send_sem=send,
            recv_sem=recv,
            device_id=device,
            device_id_type=pl.DeviceIdType.MESH,
        )
        copy.start()
        sent.append(copy)
        return copy

    def swap(number, source, land):
        copies = []
        for k in range(1, slabs):
            peer = lax.rem(me + k, slabs)
            copies.append(
                remote(
                    source.at[peer],
                    land.at[k],
                    swap_send.at[number, k],
                    swap_recv.at[number, k],
                    {"freq": peer},
                )
            )
        land[0] = source[me]
        for copy in copies:
            copy.wait_recv()

    def side(number, source, target, device):
        return remote(source, target, side_send.at[number], side_recv.at[number], device)

    def slot(source):
        return lax.rem(me - source + slabs, slabs)

    def turn_of(number):
        angle = 2.0 * math.pi * (number % slabs) / slabs
        return math.cos(angle), math.sin(angle)

    def span(s):
        return slice(s * block, (s + 1) * block)

    swap(0, src_ref, land1)
    signal = [land1[slot(s)].astype(jnp.float32) for s in range(slabs)]
    for k in range(slabs):
        re = sum(signal[s] * turn_of(s * k)[0] for s in range(slabs))
        im = -sum(signal[s] * turn_of(s * k)[1] for s in range(slabs))
        cos, sin = twist_ref[0, k], twist_ref[1, k]
        pack2[k, :block] = (re * cos + im * sin).astype(half)
        pack2[k, block:] = (im * cos - re * sin).astype(half)
    swap(1, pack2, land2)
    for s in range(slabs):
        cols_ref[0, span(s)] = land2[slot(s), :block]
        cols_ref[1, span(s)] = land2[slot(s), block:]
    cos_long, sin_long = cos_ref[...], sin_ref[...]
    col_re, col_im = cols_ref[0], cols_ref[1]
    freq_re = matmul(cos_long, col_re) + matmul(sin_long, col_im)
    freq_im = matmul(cos_long, col_im) - matmul(sin_long, col_re)
    coef_re, coef_im = filter_ref[0].astype(jnp.float32), filter_ref[1].astype(jnp.float32)
    shaped_re = (coef_re * freq_re - coef_im * freq_im).astype(half)
    shaped_im = (coef_re * freq_im + coef_im * freq_re).astype(half)
    back_re = matmul(cos_long, shaped_re) - matmul(sin_long, shaped_im)
    back_im = matmul(cos_long, shaped_im) + matmul(sin_long, shaped_re)
    spun_re = (back_re * undo_ref[0] - back_im * undo_ref[1]).astype(half)
    spun_im = (back_im * undo_ref[0] + back_re * undo_ref[1]).astype(half)
    for s in range(slabs):
        pack3[s, :block] = spun_re[span(s)]
        pack3[s, block:] = spun_im[span(s)]
    swap(2, pack3, land3)
    real = [land3[slot(k), :block].astype(jnp.float32) for k in range(slabs)]
    imag = [land3[slot(k), block:].astype(jnp.float32) for k in range(slabs)]
    for s in range(slabs):
        pack4[s] = sum(
            real[k] * turn_of(s * k)[0] - imag[k] * turn_of(s * k)[1] for k in range(slabs)
        ).astype(half)
    swap(3, pack4, land4)
    for s in range(slabs):
        mixed = src_ref[s].astype(jnp.float32) + land4[slot(s)].astype(jnp.float32) / (length * slabs)
        mixed_ref[span(s)] = mixed
        rows_ref[mine, span(s)] = mixed.astype(half)

    to_cross = side(0, rows_ref.at[mine], rows_ref.at[mine], {"chan": 1 - chan})
    to_sibling = side(1, rows_ref.at[mine], rows_ref.at[mine], {"expert": 1 - core})
    to_cross.wait_recv()
    forward = side(2, rows_ref.at[other], rows_ref.at[other], {"expert": 1 - core})
    to_sibling.wait_recv()
    forward.wait_recv()
    quarters = [rows_ref[q].astype(jnp.float32) for q in range(4)]
    total = sum(jnp.sum(x * x, axis=-1, keepdims=True) for x in quarters)
    scale = lax.rsqrt(total / (4 * width) + EPS)
    for q in range(4):
        cols = slice(q * width, (q + 1) * width)
        normed_ref[:, cols] = (quarters[q] * scale * gain_ref[:, cols]).astype(half)
    for load in loads:
        load.wait()
    gate = matmul(normed_ref[...], gate_ref[...])
    up = matmul(normed_ref[...], up_ref[...])
    hidden = (gate / (1.0 + jnp.exp(-gate)) * up).astype(half)
    for q in range(4):
        part_ref[q] = matmul(hidden, down_ref[:, q * width : (q + 1) * width]).astype(half)
    pairs = [
        side(3 + c, part_ref.at[c * 2 + 1 - core], pair_ref.at[c], {"expert": 1 - core}) for c in range(2)
    ]
    for copy in pairs:
        copy.wait_recv()

    def both(q, c):
        return part_ref[q].astype(jnp.float32) + pair_ref[c].astype(jnp.float32)

    turn_ref[...] = both(other, 1 - chan).astype(half)
    cross = side(5, turn_ref, cross_ref, {"chan": 1 - chan})
    near = mixed_ref[...] + both(mine, chan)
    cross.wait_recv()
    out_ref[...] = near + cross_ref[...].astype(jnp.float32)
    for copy in sent:
        copy.wait_send()


def encode_direct(spectra, filter_pair, gain, gate_w, up_w, down_w):
    slabs = lax.axis_size("freq")
    my_slab = lax.axis_index("freq")
    length, width = spectra.shape
    block = length // slabs
    half = jnp.bfloat16
    cos_long, sin_long = tables(length, length, length, 0)
    twist = jnp.stack(tables(slabs, block, length * slabs, my_slab * block))[..., None]
    undo = jnp.stack(tables(length, 1, length * slabs, my_slab))
    dma = pltpu.SemaphoreType.DMA
    vmem = pl.BlockSpec(memory_space=pltpu.VMEM)
    hbm = pl.BlockSpec(memory_space=pl.ANY)
    one, two = (slabs, block, width), (slabs, 2 * block, width)
    return pl.pallas_call(
        functools.partial(encode_kernel, slabs),
        out_shape=jax.ShapeDtypeStruct((length, width), jnp.float32),
        in_specs=[vmem] * 7 + [hbm] * 3,
        out_specs=vmem,
        scratch_shapes=[
            pltpu.VMEM(gate_w.shape, half),
            pltpu.VMEM(up_w.shape, half),
            pltpu.VMEM(down_w.shape, half),
            pltpu.VMEM(one, half),
            pltpu.VMEM(two, half),
            pltpu.VMEM(two, half),
            pltpu.VMEM((2, length, width), half),
            pltpu.VMEM(two, half),
            pltpu.VMEM(two, half),
            pltpu.VMEM(one, half),
            pltpu.VMEM(one, half),
            pltpu.VMEM((length, width), jnp.float32),
            pltpu.VMEM((4, length, width), half),
            pltpu.VMEM((length, 4 * width), half),
            pltpu.VMEM((4, length, width), half),
            pltpu.VMEM((2, length, width), half),
            pltpu.VMEM((length, width), half),
            pltpu.VMEM((length, width), half),
            dma((3,)),
            dma((4, slabs)),
            dma((4, slabs)),
            dma((6,)),
            dma((6,)),
        ],
        compiler_params=pltpu.CompilerParams(
            collective_id=2, has_side_effects=True, vmem_limit_bytes=28 * 1024 * 1024
        ),
    )(
        spectra.reshape(one),
        filter_pair[:, :, 0],
        cos_long.astype(half),
        sin_long.astype(half),
        twist,
        undo,
        gain[None],
        gate_w,
        up_w,
        down_w,
    )


def encode_plain(spectra, spectral_filter, norm_gain, mlp_gate, mlp_up, mlp_down):
    signal = spectra.astype(jnp.float32)
    mixed_sum = signal + spectral_mix(signal, spectral_filter)
    full_rows = lax.all_gather(
        mixed_sum.astype(jnp.bfloat16), ("chan", "expert"), axis=1, tiled=True
    )
    hidden = gated(rms_rows(full_rows, norm_gain), mlp_gate, mlp_up)
    return mixed_sum + lax.psum_scatter(
        matmul(hidden, mlp_down).astype(jnp.bfloat16),
        ("chan", "expert"),
        scatter_dimension=1,
        tiled=True,
    ).astype(jnp.float32)


def body(
    spectra,
    spectral_filter,
    norm_gain,
    mlp_gate,
    mlp_up,
    mlp_down,
    expert_gain,
    expert_gate,
    expert_up,
    expert_down,
    routes,
    combine,
):
    by_four = lax.axis_size("chan") == 2 and lax.axis_size("expert") == 2
    encode = encode_direct if by_four and spectra.shape[0] % (16 * lax.axis_size("freq")) == 0 else encode_plain
    encoded = encode(spectra, spectral_filter, norm_gain, mlp_gate, mlp_up, mlp_down)
    encoded_half = encoded.astype(jnp.bfloat16)
    slabs = lax.axis_size("freq")
    length = spectra.shape[0]
    capacity = min(length, 4 * length // slabs)
    slots_all = slabs * capacity
    picks = routes.reshape(-1)
    onehot = (picks[:, None] == lax.broadcasted_iota(jnp.int32, (1, slabs), 1)).astype(jnp.int32)
    order = lax.broadcasted_iota(jnp.int32, (picks.shape[0], picks.shape[0]), 0)
    before = order > lax.broadcasted_iota(jnp.int32, order.shape, 1)
    earlier = matmul(before.astype(jnp.bfloat16), onehot.astype(jnp.bfloat16))
    position = jnp.sum(earlier.astype(jnp.int32) * onehot, axis=1)
    slot_ids = picks * capacity + position
    placed = lax.broadcasted_iota(jnp.int32, (slots_all, 1), 0) == slot_ids[None, :]
    placed = placed.reshape(slots_all, length, 2)
    send_table = jnp.any(placed, axis=2).astype(jnp.bfloat16)
    shares = combine.astype(jnp.float32) / 8.0
    merge_table = jnp.sum(jnp.where(placed, shares[None], 0.0), axis=2).astype(jnp.bfloat16)
    outgoing = matmul(send_table, encoded_half).astype(jnp.bfloat16)
    outgoing = outgoing.reshape(slabs, capacity, -1)
    direct = (
        lax.axis_size("chan") == 2
        and lax.axis_size("expert") == 2
        and capacity % 16 == 0
        and slabs % max(1, 256 // capacity) == 0
    )
    experts = experts_direct if direct else experts_plain
    returned = experts(outgoing, expert_gain, expert_gate, expert_up, expert_down).reshape(slots_all, -1)
    routed_sum = lax.dot_general(
        merge_table, returned, (((0,), (0,)), ((), ())), preferred_element_type=jnp.float32
    )
    return (encoded + routed_sum).astype(jnp.bfloat16)


def solution(mesh):
    placed = (
        P("freq", ("chan", "expert")),
        P(None, None, "freq", ("chan", "expert")),
        P(),
        P(None, ("chan", "expert")),
        P(None, ("chan", "expert")),
        P(("chan", "expert"), None),
        P(),
        P("freq", None, ("chan", "expert")),
        P("freq", None, ("chan", "expert")),
        P("freq", ("chan", "expert"), None),
        P("freq", None),
        P("freq", None),
    )
    return jax.shard_map(
        body, mesh=mesh, in_specs=placed, out_specs=P("freq", ("chan", "expert")), check_vma=False
    )
```

```python
import functools
import math

import jax
import jax.numpy as jnp
import numpy as np
from jax import lax
from jax.experimental import pallas as pl
from jax.experimental.pallas import tpu as pltpu
from jax.sharding import PartitionSpec as P

EPS = 1e-06


def tables(height, breadth, modulus, col_start):
    left = lax.broadcasted_iota(jnp.int32, (height, breadth), 0)
    right = lax.broadcasted_iota(jnp.int32, (height, breadth), 1) + col_start
    angle = (left * right % modulus).astype(jnp.float32) * (2.0 * math.pi / modulus)
    return (jnp.cos(angle), jnp.sin(angle))


def precise(left, right):
    return matmul(left.astype(jnp.bfloat16), right.astype(jnp.bfloat16))


def matmul(left, right):
    return jnp.dot(left, right, preferred_element_type=jnp.float32)


def rms_rows(values, gain_vec):
    values = values.astype(jnp.float32)
    inverse_rms = lax.rsqrt(jnp.mean(values * values, axis=-1, keepdims=True) + EPS)
    return (values * inverse_rms * gain_vec).astype(jnp.bfloat16)


def gated(normed, gate_w, up_w):
    return (jax.nn.silu(matmul(normed, gate_w)) * matmul(normed, up_w)).astype(jnp.bfloat16)


def across_slabs(values):
    return lax.all_to_all(
        values.astype(jnp.bfloat16), "freq", split_axis=0, concat_axis=0, tiled=True
    ).astype(values.dtype)


def spectral_mix(signal, filter_pair):
    slabs = lax.axis_size("freq")
    length = signal.shape[0]
    channels = signal.shape[1]
    block_rows = length // slabs
    length_all = length * slabs
    my_slab = lax.axis_index("freq")
    cos_slab, sin_slab = tables(slabs, slabs, slabs, 0)
    cos_long, sin_long = tables(length, length, length, 0)
    gathered = across_slabs(signal).reshape(slabs, block_rows * channels)
    first_re = precise(cos_slab, gathered).reshape(slabs, block_rows, channels)
    first_im = -precise(sin_slab, gathered).reshape(slabs, block_rows, channels)
    twist_cos, twist_sin = tables(slabs, block_rows, length_all, my_slab * block_rows)
    twist_cos = twist_cos[:, :, None]
    twist_sin = twist_sin[:, :, None]
    turned_re = first_re * twist_cos + first_im * twist_sin
    turned_im = first_im * twist_cos - first_re * twist_sin
    packed = jnp.stack([turned_re, turned_im], axis=2).reshape(length, 2, channels)
    columns = across_slabs(packed)
    col_re = columns[:, 0]
    col_im = columns[:, 1]
    freq_re = precise(cos_long, col_re) + precise(sin_long, col_im)
    freq_im = precise(cos_long, col_im) - precise(sin_long, col_re)
    coef_re = filter_pair[0, :, 0].astype(jnp.float32)
    coef_im = filter_pair[1, :, 0].astype(jnp.float32)
    shaped_re = coef_re * freq_re - coef_im * freq_im
    shaped_im = coef_re * freq_im + coef_im * freq_re
    back_re = precise(cos_long, shaped_re) - precise(sin_long, shaped_im)
    back_im = precise(cos_long, shaped_im) + precise(sin_long, shaped_re)
    undo_cos, undo_sin = tables(length, 1, length_all, my_slab)
    spun_re = back_re * undo_cos - back_im * undo_sin
    spun_im = back_im * undo_cos + back_re * undo_sin
    packed_back = jnp.stack([spun_re, spun_im], axis=1)
    rows_back = across_slabs(packed_back).reshape(slabs, block_rows, 2, channels)
    real_rows = rows_back[:, :, 0].reshape(slabs, block_rows * channels)
    imag_rows = rows_back[:, :, 1].reshape(slabs, block_rows * channels)
    spatial = precise(cos_slab, real_rows) - precise(sin_slab, imag_rows)
    spatial = spatial.reshape(length, channels)
    return across_slabs(spatial) / length_all


def experts_kernel(
    slabs,
    per,
    out_ref_rows,
    gain_ref,
    gate_hbm,
    up_hbm,
    down_hbm,
    back_ref,
    gate_ref,
    up_ref,
    down_ref,
    rows_ref,
    normed_ref,
    hidden_ref,
    part_ref,
    pair_ref,
    turn_ref,
    cross_ref,
    final_ref,
    ret_ref,
    weight_sem,
    disp_send,
    disp_recv,
    x_send,
    x_recv,
    sib_send,
    sib_recv,
    fwd_send,
    fwd_recv,
    pair_send,
    pair_recv,
    cross_send,
    cross_recv,
    ret_send,
    ret_recv,
):
    me = lax.axis_index("freq")
    chan = lax.axis_index("chan")
    core = lax.axis_index("expert")
    mine = chan * 2 + core
    other = (1 - chan) * 2 + core
    groups = slabs // per
    capacity, width = rows_ref.shape[2], rows_ref.shape[3]
    rows = per * capacity

    loads = [
        pltpu.make_async_copy(source, target, weight_sem.at[number])
        for number, (source, target) in enumerate(
            ((gate_hbm, gate_ref), (up_hbm, up_ref), (down_hbm, down_ref))
        )
    ]
    for load in loads:
        load.start()

    def remote(source, target, send, recv, device):
        return pltpu.make_async_remote_copy(
            src_ref=source,
            dst_ref=target,
            send_sem=send,
            recv_sem=recv,
            device_id=device,
            device_id_type=pl.DeviceIdType.MESH,
        )

    def dispatch(k):
        peer = lax.rem(me + k, slabs)
        return remote(
            out_ref_rows.at[peer], rows_ref.at[mine, k], disp_send.at[k], disp_recv.at[k], {"freq": peer}
        )

    def span(i):
        return pl.ds(i * per, per)

    def to_cross(i):
        block = rows_ref.at[mine, span(i)]
        return remote(block, block, x_send.at[i], x_recv.at[i], {"chan": 1 - chan})

    def from_cross(i):
        block = rows_ref.at[other, span(i)]
        return remote(block, block, x_send.at[i], x_recv.at[i], {"chan": 1 - chan})

    def to_sibling(i):
        block = rows_ref.at[mine, span(i)]
        return remote(block, block, sib_send.at[i], sib_recv.at[i], {"expert": 1 - core})

    def forward(i):
        block = rows_ref.at[other, span(i)]
        return remote(block, block, fwd_send.at[i], fwd_recv.at[i], {"expert": 1 - core})

    def pair(c, i):
        return remote(
            part_ref.at[c * 2 + 1 - core, span(i)],
            pair_ref.at[c, span(i)],
            pair_send.at[c, i],
            pair_recv.at[c, i],
            {"expert": 1 - core},
        )

    def cross(i):
        return remote(
            turn_ref.at[span(i)], cross_ref.at[span(i)], cross_send.at[i], cross_recv.at[i], {"chan": 1 - chan}
        )

    def give_back(k):
        home = lax.rem(me - k + slabs, slabs)
        return remote(final_ref.at[k], ret_ref.at[k], ret_send.at[k], ret_recv.at[k], {"freq": home})

    def arrive(i):
        for j in range(per):
            k = i * per + j

            @pl.when(k > 0)
            def _():
                dispatch(k).wait_recv()

        to_cross(i).start()
        to_sibling(i).start()

    def pass_on(i):
        from_cross(i).wait_recv()
        forward(i).start()

    def compute(i):
        to_sibling(i).wait_recv()
        forward(i).wait_recv()
        quarters = [
            rows_ref[q, span(i)].reshape(rows, width).astype(jnp.float32) for q in range(4)
        ]
        total = sum(jnp.sum(x * x, axis=-1, keepdims=True) for x in quarters)
        scale = lax.rsqrt(total / (4 * width) + EPS)
        for q in range(4):
            cols = slice(q * width, (q + 1) * width)
            normed_ref[:, cols] = (quarters[q] * scale * gain_ref[:, cols]).astype(jnp.bfloat16)

        @pl.when(i == 0)
        def _():
            for load in loads:
                load.wait()

        tile = 256
        for start in range(0, hidden_ref.shape[1], tile):
            cols = slice(start, start + tile)
            gate = matmul(normed_ref[...], gate_ref[0, :, cols])
            up = matmul(normed_ref[...], up_ref[0, :, cols])
            hidden_ref[:, cols] = (gate / (1.0 + jnp.exp(-gate)) * up).astype(jnp.bfloat16)
        for q in range(4):
            part = matmul(hidden_ref[...], down_ref[0, :, q * width : (q + 1) * width])
            part_ref[q, span(i)] = part.astype(jnp.bfloat16).reshape(per, capacity, width)
        pair(0, i).start()
        pair(1, i).start()

    def both(q, c, i):
        return part_ref[q, span(i)].astype(jnp.float32) + pair_ref[c, span(i)].astype(jnp.float32)

    def turn(i):
        pair(0, i).wait_recv()
        pair(1, i).wait_recv()
        turn_ref[span(i)] = both(other, 1 - chan, i).astype(jnp.bfloat16)
        cross(i).start()

    def finish(i):
        cross(i).wait_recv()
        final_ref[span(i)] = (both(mine, chan, i) + cross_ref[span(i)].astype(jnp.float32)).astype(
            jnp.bfloat16
        )
        for j in range(per):
            k = i * per + j

            @pl.when(k > 0)
            def _():
                give_back(k).start()

    for k in range(1, slabs):
        dispatch(k).start()
    rows_ref[mine, 0] = out_ref_rows[me]
    arrive(0)
    pass_on(0)

    def step(i, carry):
        @pl.when(i + 1 < groups)
        def _():
            arrive(i + 1)

        compute(i)

        @pl.when(i + 1 < groups)
        def _():
            pass_on(i + 1)

        @pl.when(i >= 1)
        def _():
            turn(i - 1)

        @pl.when(i >= 2)
        def _():
            finish(i - 2)

        return carry

    lax.fori_loop(0, groups, step, 0)
    turn(groups - 1)
    if groups >= 2:
        finish(groups - 2)
    finish(groups - 1)
    back_ref[me] = final_ref[0]
    for k in range(1, slabs):
        give_back(k).wait_recv()
        back_ref[lax.rem(me + k, slabs)] = ret_ref[k]
    for k in range(1, slabs):
        dispatch(k).wait_send()
        give_back(k).wait_send()
    for i in range(groups):
        to_cross(i).wait_send()
        to_sibling(i).wait_send()
        forward(i).wait_send()
        pair(0, i).wait_send()
        pair(1, i).wait_send()
        cross(i).wait_send()


def experts_plain(outgoing, gain, gate_w, up_w, down_w):
    slabs, capacity, width = outgoing.shape
    arrived = lax.all_to_all(outgoing, "freq", split_axis=0, concat_axis=0, tiled=True)
    arrived = lax.all_gather(arrived, ("chan", "expert"), axis=2, tiled=True).reshape(slabs * capacity, -1)
    expert_hidden = gated(rms_rows(arrived, gain), gate_w[0], up_w[0])
    expert_out = lax.psum_scatter(
        matmul(expert_hidden, down_w[0]).astype(jnp.bfloat16), ("chan", "expert"), scatter_dimension=1, tiled=True
    ).reshape(slabs, capacity, width)
    return lax.all_to_all(expert_out, "freq", split_axis=0, concat_axis=0, tiled=True)


def encode_kernel(
    slabs,
    src_ref,
    filter_ref,
    cos_ref,
    sin_ref,
    twist_ref,
    undo_ref,
    gain_ref,
    gate_hbm,
    up_hbm,
    down_hbm,
    out_ref,
    gate_ref,
    up_ref,
    down_ref,
    land1,
    pack2,
    land2,
    cols_ref,
    pack3,
    land3,
    pack4,
    land4,
    mixed_ref,
    rows_ref,
    normed_ref,
    part_ref,
    pair_ref,
    turn_ref,
    cross_ref,
    weight_sem,
    swap_send,
    swap_recv,
    side_send,
    side_recv,
):
    me = lax.axis_index("freq")
    chan = lax.axis_index("chan")
    core = lax.axis_index("expert")
    mine = chan * 2 + core
    other = (1 - chan) * 2 + core
    block, width = src_ref.shape[1], src_ref.shape[2]
    length = slabs * block
    half = jnp.bfloat16
    loads = [
        pltpu.make_async_copy(source, target, weight_sem.at[number])
        for number, (source, target) in enumerate(
            ((gate_hbm, gate_ref), (up_hbm, up_ref), (down_hbm, down_ref))
        )
    ]
    for load in loads:
        load.start()
    barrier = pltpu.get_barrier_semaphore()
    for k in range(1, slabs):
        pl.semaphore_signal(
            barrier, inc=1, device_id={"freq": lax.rem(me + k, slabs)}, device_id_type=pl.DeviceIdType.MESH
        )
    pl.semaphore_signal(barrier, inc=1, device_id={"chan": 1 - chan}, device_id_type=pl.DeviceIdType.MESH)
    pl.semaphore_signal(barrier, inc=1, device_id={"expert": 1 - core}, device_id_type=pl.DeviceIdType.MESH)
    pl.semaphore_wait(barrier, slabs + 1)
    sent = []

    def remote(source, target, send, recv, device):
        copy = pltpu.make_async_remote_copy(
            src_ref=source,
            dst_ref=target,
            send_sem=send,
            recv_sem=recv,
            device_id=device,
            device_id_type=pl.DeviceIdType.MESH,
        )
        copy.start()
        sent.append(copy)
        return copy

    def swap(number, source, land):
        copies = []
        for k in range(1, slabs):
            peer = lax.rem(me + k, slabs)
            copies.append(
                remote(
                    source.at[peer],
                    land.at[k],
                    swap_send.at[number, k],
                    swap_recv.at[number, k],
                    {"freq": peer},
                )
            )
        land[0] = source[me]
        for copy in copies:
            copy.wait_recv()

    def side(number, source, target, device):
        return remote(source, target, side_send.at[number], side_recv.at[number], device)

    def slot(source):
        return lax.rem(me - source + slabs, slabs)

    def turn_of(number):
        angle = 2.0 * math.pi * (number % slabs) / slabs
        return math.cos(angle), math.sin(angle)

    def span(s):
        return slice(s * block, (s + 1) * block)

    swap(0, src_ref, land1)
    signal = [land1[slot(s)].astype(jnp.float32) for s in range(slabs)]
    for k in range(slabs):
        re = sum(signal[s] * turn_of(s * k)[0] for s in range(slabs))
        im = -sum(signal[s] * turn_of(s * k)[1] for s in range(slabs))
        cos, sin = twist_ref[0, k], twist_ref[1, k]
        pack2[k, :block] = (re * cos + im * sin).astype(half)
        pack2[k, block:] = (im * cos - re * sin).astype(half)
    swap(1, pack2, land2)
    for s in range(slabs):
        cols_ref[0, span(s)] = land2[slot(s), :block]
        cols_ref[1, span(s)] = land2[slot(s), block:]
    cos_long, sin_long = cos_ref[...], sin_ref[...]
    col_re, col_im = cols_ref[0], cols_ref[1]
    freq_re = matmul(cos_long, col_re) + matmul(sin_long, col_im)
    freq_im = matmul(cos_long, col_im) - matmul(sin_long, col_re)
    coef_re, coef_im = filter_ref[0].astype(jnp.float32), filter_ref[1].astype(jnp.float32)
    shaped_re = (coef_re * freq_re - coef_im * freq_im).astype(half)
    shaped_im = (coef_re * freq_im + coef_im * freq_re).astype(half)
    back_re = matmul(cos_long, shaped_re) - matmul(sin_long, shaped_im)
    back_im = matmul(cos_long, shaped_im) + matmul(sin_long, shaped_re)
    spun_re = (back_re * undo_ref[0] - back_im * undo_ref[1]).astype(half)
    spun_im = (back_im * undo_ref[0] + back_re * undo_ref[1]).astype(half)
    for s in range(slabs):
        pack3[s, :block] = spun_re[span(s)]
        pack3[s, block:] = spun_im[span(s)]
    swap(2, pack3, land3)
    real = [land3[slot(k), :block].astype(jnp.float32) for k in range(slabs)]
    imag = [land3[slot(k), block:].astype(jnp.float32) for k in range(slabs)]
    for s in range(slabs):
        pack4[s] = sum(
            real[k] * turn_of(s * k)[0] - imag[k] * turn_of(s * k)[1] for k in range(slabs)
        ).astype(half)
    swap(3, pack4, land4)
    for s in range(slabs):
        mixed = src_ref[s].astype(jnp.float32) + land4[slot(s)].astype(jnp.float32) / (length * slabs)
        mixed_ref[span(s)] = mixed
        rows_ref[mine, span(s)] = mixed.astype(half)

    to_cross = side(0, rows_ref.at[mine], rows_ref.at[mine], {"chan": 1 - chan})
    to_sibling = side(1, rows_ref.at[mine], rows_ref.at[mine], {"expert": 1 - core})
    to_cross.wait_recv()
    forward = side(2, rows_ref.at[other], rows_ref.at[other], {"expert": 1 - core})
    to_sibling.wait_recv()
    forward.wait_recv()
    quarters = [rows_ref[q].astype(jnp.float32) for q in range(4)]
    total = sum(jnp.sum(x * x, axis=-1, keepdims=True) for x in quarters)
    scale = lax.rsqrt(total / (4 * width) + EPS)
    for q in range(4):
        cols = slice(q * width, (q + 1) * width)
        normed_ref[:, cols] = (quarters[q] * scale * gain_ref[:, cols]).astype(half)
    for load in loads:
        load.wait()
    gate = matmul(normed_ref[...], gate_ref[...])
    up = matmul(normed_ref[...], up_ref[...])
    hidden = (gate / (1.0 + jnp.exp(-gate)) * up).astype(half)
    for q in range(4):
        part_ref[q] = matmul(hidden, down_ref[:, q * width : (q + 1) * width]).astype(half)
    pairs = [
        side(3 + c, part_ref.at[c * 2 + 1 - core], pair_ref.at[c], {"expert": 1 - core}) for c in range(2)
    ]
    for copy in pairs:
        copy.wait_recv()

    def both(q, c):
        return part_ref[q].astype(jnp.float32) + pair_ref[c].astype(jnp.float32)

    turn_ref[...] = both(other, 1 - chan).astype(half)
    cross = side(5, turn_ref, cross_ref, {"chan": 1 - chan})
    near = mixed_ref[...] + both(mine, chan)
    cross.wait_recv()
    out_ref[...] = near + cross_ref[...].astype(jnp.float32)
    for copy in sent:
        copy.wait_send()


def layer_kernel(slabs, per, split, *refs):
    encode_in, (table_ref, gain_ref), weights = refs[:10], refs[10:12], refs[12:15]
    (encoded_ref, back_ref), scratch = refs[15:17], refs[17:]
    encode_kernel(slabs, *encode_in, encoded_ref, *scratch[:split])
    outgoing_ref = scratch[split]
    half = encoded_ref[...].astype(jnp.bfloat16)
    for k in range(slabs):
        outgoing_ref[k] = matmul(table_ref[k], half).astype(jnp.bfloat16)
    experts_kernel(slabs, per, outgoing_ref, gain_ref, *weights, back_ref, *scratch[split + 1 :])


def layer_direct(spectra, filter_pair, gain, gate_w, up_w, down_w, send_table, egain, egate, eup, edown):
    slabs = lax.axis_size("freq")
    my_slab = lax.axis_index("freq")
    length, width = spectra.shape
    capacity = send_table.shape[0] // slabs
    per = max(1, 256 // capacity)
    groups = slabs // per
    hidden = egate.shape[2]
    block = length // slabs
    half = jnp.bfloat16
    steps = np.arange(length)
    angle = (steps[:, None] * steps[None, :] % length) * (2.0 * math.pi / length)
    twist = jnp.stack(tables(slabs, block, length * slabs, my_slab * block))[..., None]
    undo = jnp.stack(tables(length, 1, length * slabs, my_slab))
    dma = pltpu.SemaphoreType.DMA
    vmem = pl.BlockSpec(memory_space=pltpu.VMEM)
    hbm = pl.BlockSpec(memory_space=pl.ANY)
    one, two = (slabs, block, width), (slabs, 2 * block, width)
    encode_scratch = [
            pltpu.VMEM(gate_w.shape, half),
            pltpu.VMEM(up_w.shape, half),
            pltpu.VMEM(down_w.shape, half),
            pltpu.VMEM(one, half),
            pltpu.VMEM(two, half),
            pltpu.VMEM(two, half),
            pltpu.VMEM((2, length, width), half),
            pltpu.VMEM(two, half),
            pltpu.VMEM(two, half),
            pltpu.VMEM(one, half),
            pltpu.VMEM(one, half),
            pltpu.VMEM((length, width), jnp.float32),
            pltpu.VMEM((4, length, width), half),
            pltpu.VMEM((length, 4 * width), half),
            pltpu.VMEM((4, length, width), half),
            pltpu.VMEM((2, length, width), half),
            pltpu.VMEM((length, width), half),
            pltpu.VMEM((length, width), half),
            dma((3,)),
            dma((4, slabs)),
            dma((4, slabs)),
            dma((6,)),
            dma((6,)),
        ]
    expert_scratch = [
            pltpu.VMEM(egate.shape, half),
            pltpu.VMEM(eup.shape, half),
            pltpu.VMEM(edown.shape, half),
            pltpu.VMEM((4, slabs, capacity, width), half),
            pltpu.VMEM((per * capacity, 4 * width), half),
            pltpu.VMEM((per * capacity, hidden), half),
            pltpu.VMEM((4, slabs, capacity, width), half),
            pltpu.VMEM((2, slabs, capacity, width), half),
            pltpu.VMEM((slabs, capacity, width), half),
            pltpu.VMEM((slabs, capacity, width), half),
            pltpu.VMEM((slabs, capacity, width), half),
            pltpu.VMEM((slabs, capacity, width), half),
            dma((3,)),
            dma((slabs,)),
            dma((slabs,)),
            dma((groups,)),
            dma((groups,)),
            dma((groups,)),
            dma((groups,)),
            dma((groups,)),
            dma((groups,)),
            dma((2, groups)),
            dma((2, groups)),
            dma((groups,)),
            dma((groups,)),
            dma((slabs,)),
            dma((slabs,)),
        ]
    slots = (slabs, capacity, width)
    return pl.pallas_call(
        functools.partial(layer_kernel, slabs, per, len(encode_scratch)),
        out_shape=(jax.ShapeDtypeStruct((length, width), jnp.float32), jax.ShapeDtypeStruct(slots, half)),
        in_specs=[vmem] * 7 + [hbm] * 3 + [vmem] * 2 + [hbm] * 3,
        out_specs=(vmem, vmem),
        scratch_shapes=encode_scratch + [pltpu.VMEM(slots, half)] + expert_scratch,
        compiler_params=pltpu.CompilerParams(
            collective_id=2, has_side_effects=True, vmem_limit_bytes=48 * 1024 * 1024
        ),
    )(
        spectra.reshape(one),
        filter_pair[:, :, 0],
        jnp.asarray(np.cos(angle), half),
        jnp.asarray(np.sin(angle), half),
        twist,
        undo,
        gain[None],
        gate_w,
        up_w,
        down_w,
        send_table.reshape(slabs, capacity, length),
        egain[None],
        egate,
        eup,
        edown,
    )


def encode_plain(spectra, spectral_filter, norm_gain, mlp_gate, mlp_up, mlp_down):
    signal = spectra.astype(jnp.float32)
    mixed_sum = signal + spectral_mix(signal, spectral_filter)
    full_rows = lax.all_gather(
        mixed_sum.astype(jnp.bfloat16), ("chan", "expert"), axis=1, tiled=True
    )
    hidden = gated(rms_rows(full_rows, norm_gain), mlp_gate, mlp_up)
    return mixed_sum + lax.psum_scatter(
        matmul(hidden, mlp_down).astype(jnp.bfloat16),
        ("chan", "expert"),
        scatter_dimension=1,
        tiled=True,
    ).astype(jnp.float32)


def body(
    spectra,
    spectral_filter,
    norm_gain,
    mlp_gate,
    mlp_up,
    mlp_down,
    expert_gain,
    expert_gate,
    expert_up,
    expert_down,
    routes,
    combine,
):
    slabs = lax.axis_size("freq")
    length = spectra.shape[0]
    capacity = min(length, 4 * length // slabs)
    slots_all = slabs * capacity
    picks = routes.reshape(-1)
    onehot = (picks[:, None] == lax.broadcasted_iota(jnp.int32, (1, slabs), 1)).astype(jnp.int32)
    order = lax.broadcasted_iota(jnp.int32, (picks.shape[0], picks.shape[0]), 0)
    before = order > lax.broadcasted_iota(jnp.int32, order.shape, 1)
    earlier = matmul(before.astype(jnp.bfloat16), onehot.astype(jnp.bfloat16))
    position = jnp.sum(earlier.astype(jnp.int32) * onehot, axis=1)
    slot_ids = picks * capacity + position
    placed = lax.broadcasted_iota(jnp.int32, (slots_all, 1), 0) == slot_ids[None, :]
    placed = placed.reshape(slots_all, length, 2)
    send_table = jnp.any(placed, axis=2).astype(jnp.bfloat16)
    shares = combine.astype(jnp.float32) / 8.0
    merge_table = jnp.sum(jnp.where(placed, shares[None], 0.0), axis=2).astype(jnp.bfloat16)
    encoder = (spectra, spectral_filter, norm_gain, mlp_gate, mlp_up, mlp_down)
    experts = (expert_gain, expert_gate, expert_up, expert_down)
    direct = (
        lax.axis_size("chan") == 2
        and lax.axis_size("expert") == 2
        and length % (16 * slabs) == 0
        and capacity % 16 == 0
        and slabs % max(1, 256 // capacity) == 0
    )
    if direct:
        encoded, returned = layer_direct(*encoder, send_table, *experts)
    else:
        encoded = encode_plain(*encoder)
        outgoing = matmul(send_table, encoded.astype(jnp.bfloat16)).astype(jnp.bfloat16)
        returned = experts_plain(outgoing.reshape(slabs, capacity, -1), *experts)
    returned = returned.reshape(slots_all, -1)
    routed_sum = lax.dot_general(
        merge_table, returned, (((0,), (0,)), ((), ())), preferred_element_type=jnp.float32
    )
    return (encoded + routed_sum).astype(jnp.bfloat16)


def solution(mesh):
    placed = (
        P("freq", ("chan", "expert")),
        P(None, None, "freq", ("chan", "expert")),
        P(),
        P(None, ("chan", "expert")),
        P(None, ("chan", "expert")),
        P(("chan", "expert"), None),
        P(),
        P("freq", None, ("chan", "expert")),
        P("freq", None, ("chan", "expert")),
        P("freq", ("chan", "expert"), None),
        P("freq", None),
        P("freq", None),
    )
    return jax.shard_map(
        body, mesh=mesh, in_specs=placed, out_specs=P("freq", ("chan", "expert")), check_vma=False
    )
```
